32 devices in a mesh: dp: 16 (over z, x, core), tensor: 2 (over y).
Axes of the slice: x: 2, y: 2, z: 4, core: 2. Of those that a mesh axis runs over, the one named last changes fastest.
Arguments:
- tokens: bfloat16 [32768, 768], P(('dp', 'tensor')), may hold values from -6 to 6
- teacher: bfloat16 [32768, 768], P(('dp', 'tensor')), may hold values from -23 to 23
- segments: int32 [64, 512], P(('dp', 'tensor')), may hold values from 0 to 3, never falling along the last dimension, each value on 1 to 256 neighbouring positions
- qkv_weight: bfloat16 [768, 3, 768], P('dp', None, 'tensor'), may hold values from -0.21875 to 0.21875
- qkv_bias: float32 [2, 768], replicated, may hold values from -3 to 3
- out_weight: bfloat16 [768, 768], P('dp', 'tensor'), may hold values from -1.75 to 1.75
- out_bias: float32 [768], replicated, may hold values from -3 to 3
- up_weight: bfloat16 [768, 3072], P('dp', 'tensor'), may hold values from -0.21875 to 0.21875
- up_bias: float32 [3072], replicated, may hold values from -3 to 3
- down_weight: bfloat16 [768, 3072], P('dp', 'tensor'), may hold values from -0.21875 to 0.21875
- down_bias: float32 [768], replicated, may hold values from -3 to 3
- first_gain: float32 [768], replicated, may hold values from 0.5 to 1.5
- first_shift: float32 [768], replicated, may hold values from -2 to 2
- second_gain: float32 [768], replicated, may hold values from 0.5 to 1.5
- second_shift: float32 [768], replicated, may hold values from -2 to 2
- head_logit: float32 [12], replicated, may hold values from -1 to 3
- unit_logit: float32 [3072], replicated, may hold values from -1 to 3
- width_logit: float32 [768], replicated, may hold values from -1 to 3
- layer_logit: float32 [2], replicated, may hold values from -1 to 3
- head_noise: float32 [12], replicated, may hold values from 0.05 to 0.95
- unit_noise: float32 [3072], replicated, may hold values from 0.05 to 0.95
- width_noise: float32 [768], replicated, may hold values from 0.05 to 0.95
- layer_noise: float32 [2], replicated, may hold values from 0.05 to 0.95
Outputs:
- activations: bfloat16 [32768, 768], P(('dp', 'tensor'))
- distill_loss: float32 [], replicated
- tokens_grad: float32 [32768, 768], P(('dp', 'tensor'))
- qkv_weight_grad: float32 [768, 3, 768], P('dp', None, 'tensor')
- qkv_bias_grad: float32 [2, 768], replicated
- out_weight_grad: float32 [768, 768], P('dp', 'tensor')
- out_bias_grad: float32 [768], replicated
- up_weight_grad: float32 [768, 3072], P('dp', 'tensor')
- up_bias_grad: float32 [3072], replicated
- down_weight_grad: float32 [768, 3072], P('dp', 'tensor')
- down_bias_grad: float32 [768], replicated
- first_gain_grad: float32 [768], replicated
- first_shift_grad: float32 [768], replicated
- second_gain_grad: float32 [768], replicated
- second_shift_grad: float32 [768], replicated
- head_logit_grad: float32 [12], replicated
- unit_logit_grad: float32 [3072], replicated
- width_logit_grad: float32 [768], replicated
- layer_logit_grad: float32 [2], replicated
The draws below stay inside these ranges and needn't reach their ends.
Inputs may be any that keep to these rules, and one draw needn't show every extreme that they name: `segments`: each row is one sequence; its item ids never fall along the row, every id occurs in every row, and an item spans at most 256 rows.
All inputs are finite; a program needn't handle non-finite values.
Results may differ from the reference program's by a relative error of at most 0.012.
The reference program's roundings to bfloat16 on the way count: a program that leaves them out, or rounds other values in their place, can miss the bound.
Values may be sent and summed in bfloat16 or wider, within the bound.
A program may use at most 192 MiB of HBM per device.

```python
import math
from functools import partial
import jax
import jax.numpy as jnp
import numpy as np
from jax import lax

D = 768
HEADS = 12
HEAD_DIM = 64
FF = 3072
SEQ_LEN = 512
ITEMS = 4
ITEM_MOST = 256
TOKENS = 32768
SEQUENCES = 64


def draw_teacher(key, part):
    key = jax.random.fold_in(key, 7)
    row = jnp.arange(TOKENS, dtype=jnp.float32)[:, None]
    rise = 1.0 + 2.0 * row / TOKENS
    base = jnp.clip(jax.random.normal(key, (TOKENS, D), jnp.float32), -5.0, 5.0)
    return (base * rise).astype(jnp.bfloat16)


def raised(entries, rng, source, target, parts, factor):
    def block_of(position):
        return (jnp.arange(entries.shape[position]) // (entries.shape[position] // parts)).reshape((-1,) + (1,) * (entries.ndim - 1 - position))

    first = jax.random.permutation(rng, parts)[block_of(target)]
    second = (block_of(target) + parts // 2) % parts
    return jnp.where((block_of(source) == first) | (block_of(source) == second), factor * entries, entries)


def block_scale(key, extent, cuts, low, high):
    def one(axis_at, parts):
        steps = jax.random.uniform(jax.random.fold_in(jax.random.fold_in(key, 6), axis_at), (parts,), jnp.float32, low / len(cuts), high / len(cuts))
        return jnp.repeat(jnp.exp(steps), extent[axis_at] // parts).reshape((-1,) + (1,) * (len(extent) - axis_at - 1))

    level = one(*cuts[0])
    for cut in cuts[1:]:
        level = level * one(*cut)
    return level


def split_up(number_of, total, most, skew):
    weights = [(1 << 20) // math.isqrt(grade ** skew) + 1 for grade in range(2, number_of + 1)]
    spare, counts = total - most - (number_of - 1), [1] * (number_of - 1)
    while spare > 0:
        free = [i for i in range(number_of - 1) if counts[i] < most]
        pool, left = sum([weights[i] for i in free]), spare
        for i in free:
            more = min(most - counts[i], max(1, left * weights[i] // pool), spare)
            counts[i] = counts[i] + more
            spare = spare - more
    return np.array([most] + counts)


def uneven(rng, amount, total, reach, lean):
    if amount == 2:
        one = jax.random.randint(rng, (), max(1, total - reach), min(reach, total - 1) + 1)
        return jnp.stack([one, total - one])
    tallies = jnp.asarray(split_up(amount, total, reach, lean), jnp.int32)
    twos = (amount - 1) // 2
    donor, receiver = tallies[1:1 + 2 * twos:2], tallies[2:2 + 2 * twos:2]
    slack = jnp.minimum(donor - 1, reach - receiver)
    moved = jax.random.randint(jax.random.fold_in(rng, 1), (twos,), 0, 1 << 20) % (slack + 1)
    tallies = tallies.at[1:1 + 2 * twos:2].set(donor - moved).at[2:2 + 2 * twos:2].set(receiver + moved)
    return tallies[jax.random.permutation(jax.random.fold_in(rng, 2), amount)]


def bell_draw(rng, extent, width, bound, pieces=(), held_as=jnp.bfloat16):
    entries = jax.random.normal(rng, extent, jnp.float32) * width
    if len(pieces) > 0:
        entries = block_scale(rng, extent, pieces, -0.22, 0.18) * entries
    return jnp.clip(entries, min=-bound, max=bound).astype(held_as)


def bell_draw_with(rng, extent, width, most, pieces, heavy, kind=jnp.bfloat16):
    entries = width * jax.random.normal(rng, extent, jnp.float32)
    if pieces:
        entries = entries * block_scale(rng, extent, pieces, -0.22, 0.18)
    return jnp.clip(raised(entries, jax.random.fold_in(rng, 3), *heavy), -most, most).astype(kind)


def setup_inputs(seed: int = 0) -> dict:
    splits = jax.random.split(jax.random.key(seed), 24)
    tokens = bell_draw_with(splits[0], (TOKENS, D), 1.0, 6.0, ((0, 32),), (0, 1, 32, 2.75))
    teacher = draw_teacher(jax.random.fold_in(splits[23], 71), 0)
    segments = jax.vmap(lambda own: jnp.searchsorted(jnp.cumsum(uneven(own, ITEMS, SEQ_LEN, ITEM_MOST, 1)), jnp.arange(SEQ_LEN), side="right"))(jax.random.split(splits[2], SEQUENCES)).reshape((SEQUENCES, SEQ_LEN)).astype(jnp.int32)
    qkv_weight = bell_draw(splits[3], (D, 3, D), D ** -0.5, 0.21875, ((0, 16), (2, 2)))
    qkv_bias = bell_draw(splits[4], (2, D), 0.5, 3.0, (), jnp.float32)
    out_weight = bell_draw(splits[5], (D, D), (D // 64) ** -0.5, 1.75, ((0, 16), (1, 2)))
    out_bias = bell_draw(splits[6], (D,), 0.5, 3.0, (), jnp.float32)
    up_weight = bell_draw(splits[7], (D, FF), D ** -0.5, 0.21875, ((0, 16), (1, 2)))
    up_bias = bell_draw(splits[8], (FF,), 0.5, 3.0, (), jnp.float32)
    down_weight = bell_draw(splits[9], (D, FF), (FF // 4) ** -0.5, 0.21875, ((0, 16), (1, 2)))
    down_bias = bell_draw(splits[10], (D,), 0.5, 3.0, (), jnp.float32)
    first_gain = jnp.clip(1.0 + 0.1 * jax.random.normal(splits[11], (D,), jnp.float32), 0.5, 1.5)
    first_shift = bell_draw(splits[12], (D,), 0.3, 2.0, (), jnp.float32)
    second_gain = jnp.clip(1.0 + 0.1 * jax.random.normal(splits[13], (D,), jnp.float32), 0.5, 1.5)
    second_shift = bell_draw(splits[14], (D,), 0.3, 2.0, (), jnp.float32)
    head_logit = jnp.clip(jax.random.uniform(splits[15], (HEADS,), jnp.float32, -1.0, 3.0), -1.0, 3.0)
    unit_logit = jnp.clip(jax.random.uniform(splits[16], (FF,), jnp.float32, -1.0, 3.0), -1.0, 3.0)
    width_logit = jnp.clip(jax.random.uniform(splits[17], (D,), jnp.float32, -1.0, 3.0), -1.0, 3.0)
    layer_logit = jnp.clip(jax.random.uniform(splits[18], (2,), jnp.float32, -1.0, 3.0), -1.0, 3.0)
    head_noise = jnp.clip(jax.random.uniform(splits[19], (HEADS,), jnp.float32, 0.05, 0.95), 0.05, 0.95)
    unit_noise = jnp.clip(jax.random.uniform(splits[20], (FF,), jnp.float32, 0.05, 0.95), 0.05, 0.95)
    width_noise = jnp.clip(jax.random.uniform(splits[21], (D,), jnp.float32, 0.05, 0.95), 0.05, 0.95)
    layer_noise = jnp.clip(jax.random.uniform(splits[22], (2,), jnp.float32, 0.05, 0.95), 0.05, 0.95)
    return dict(tokens=tokens, teacher=teacher, segments=segments, qkv_weight=qkv_weight, qkv_bias=qkv_bias, out_weight=out_weight, out_bias=out_bias, up_weight=up_weight, up_bias=up_bias, down_weight=down_weight, down_bias=down_bias, first_gain=first_gain, first_shift=first_shift, second_gain=second_gain, second_shift=second_shift, head_logit=head_logit, unit_logit=unit_logit, width_logit=width_logit, layer_logit=layer_logit, head_noise=head_noise, unit_noise=unit_noise, width_noise=width_noise, layer_noise=layer_noise)


BETA = 2.0 / 3.0
EPS = 1e-12
NEG = -1e+30
HIGH = lax.Precision.HIGHEST

@jax.custom_vjp
def low(v):
    return lax.optimization_barrier(v.astype(jnp.bfloat16)).astype(jnp.float32)

@jax.custom_vjp
def low_back(v):
    return v

def low_keep(v):
    return (low(v), None)

def low_pass(kept, grad):
    return (grad,)

def back_keep(v):
    return (v, None)

def back_low(kept, grad):
    return (low(grad),)
low.defvjp(low_keep, low_pass)
low_back.defvjp(back_keep, back_low)

def gate_values(noise, logit):
    return jax.nn.sigmoid((jnp.log(noise) - jnp.log1p(-noise) + logit) / BETA)

def layer_norm(value, gain, shift):
    mean = lax.optimization_barrier(jnp.mean(value, axis=-1, keepdims=True))
    centred = value - mean
    var = lax.optimization_barrier(jnp.mean(centred * centred, axis=-1, keepdims=True))
    return centred * lax.rsqrt(var + EPS) * gain + shift

def matmul(left, right):
    return jnp.dot(left, right, precision=HIGH)

def block_forward(noises, params, block_rows, block_marks, block_teacher):
    qkv_weight, qkv_bias, out_weight, out_bias, up_weight, up_bias, down_weight, down_bias, first_gain, first_shift, second_gain, second_shift, head_logit, unit_logit, width_logit, layer_logit = params
    head_noise, unit_noise, width_noise, layer_noise = noises
    z_head = gate_values(head_noise, head_logit)
    z_unit = gate_values(unit_noise, unit_logit)
    z_width = gate_values(width_noise, width_logit)
    z_layer = gate_values(layer_noise, layer_logit)
    count = block_rows.shape[0]
    nseq = count // SEQ_LEN
    mixed = matmul(block_rows, qkv_weight.reshape(D, 3 * D))
    query = low(low_back(mixed[:, :D] + qkv_bias[0]) * HEAD_DIM ** (-0.5))
    keys = low(low_back(mixed[:, D:2 * D]))
    value_pre = low_back(mixed[:, 2 * D:] + qkv_bias[1])
    values = low(value_pre * jnp.repeat(z_head, HEAD_DIM))
    shape = (nseq, SEQ_LEN, HEADS, HEAD_DIM)
    scores = low_back(jnp.einsum('sqhd,skhd->shqk', query.reshape(shape), keys.reshape(shape), precision=HIGH))
    same = block_marks[:, :, None] == block_marks[:, None, :]
    scores = jnp.where(same[:, None], scores, NEG)
    top = lax.optimization_barrier(jnp.max(scores, axis=-1, keepdims=True))
    expo = jnp.exp(scores - top)
    probs = low(expo / lax.optimization_barrier(jnp.sum(expo, axis=-1, keepdims=True)))
    context = jnp.einsum('shqk,skhd->sqhd', probs, values.reshape(shape), precision=HIGH).reshape(count, D)
    context = low(low_back(context))
    attn = low_back(matmul(context, out_weight.T))
    normed = layer_norm(block_rows + (attn + out_bias) * (z_layer[0] * z_width), first_gain, first_shift)
    pre_up = low_back(matmul(low(normed), up_weight) + up_bias)
    activ = low(jax.nn.gelu(pre_up, approximate=False) * z_unit)
    ffn = low_back(matmul(activ, down_weight.T))
    result = layer_norm(normed + (ffn + down_bias) * (z_layer[1] * z_width), second_gain, second_shift)
    diff = result - block_teacher
    return (0.5 * jnp.sum(diff * diff), result)

def reference(tokens, teacher, segments, qkv_weight, qkv_bias, out_weight, out_bias, up_weight, up_bias, down_weight, down_bias, first_gain, first_shift, second_gain, second_shift, head_logit, unit_logit, width_logit, layer_logit, head_noise, unit_noise, width_noise, layer_noise):
    params = tuple((item.astype(jnp.float32) for item in (qkv_weight, qkv_bias, out_weight, out_bias, up_weight, up_bias, down_weight, down_bias, first_gain, first_shift, second_gain, second_shift, head_logit, unit_logit, width_logit, layer_logit)))
    noises = (head_noise, unit_noise, width_noise, layer_noise)
    block_count = TOKENS // (4 * SEQ_LEN)
    mark_blocks = segments.reshape(block_count, 4, SEQ_LEN)
    teacher_blocks = teacher.astype(jnp.float32).reshape(block_count, 4 * SEQ_LEN, D)
    step = jax.checkpoint(partial(block_forward, noises))

    def total(params, rows):
        row_blocks = rows.reshape(block_count, 4 * SEQ_LEN, D)

        def scan_step(carry, item):
            part_loss, result = step(params, item[0], item[1], item[2])
            return (carry + part_loss, result)
        loss, results = lax.scan(scan_step, jnp.zeros((), jnp.float32), (row_blocks, mark_blocks, teacher_blocks))
        return (loss, results.reshape(TOKENS, D))
    loss, back, results = jax.vjp(total, params, tokens.astype(jnp.float32), has_aux=True)
    grads, tokens_grad = back(jnp.ones((), jnp.float32))
    return (results.astype(jnp.bfloat16), loss / TOKENS, tokens_grad, grads[0], grads[1], grads[2], grads[3], grads[4], grads[5], grads[6], grads[7], grads[8], grads[9], grads[10], grads[11], grads[12], grads[13], grads[14], grads[15])
```

```python
import functools

import jax
import jax.numpy as jnp
from jax import lax
from jax.experimental import pallas as pl
from jax.experimental.pallas import tpu as pltpu
from jax.sharding import PartitionSpec as P

D = 768
HEADS = 12
HEAD_DIM = 64
FF = 3072
SEQ_LEN = 512
BETA = 2.0 / 3.0
EPS = 1e-12
NEG = -1e30
BF = jnp.bfloat16
F32 = jnp.float32
MESH = pl.DeviceIdType.MESH
VMEM_BYTES = 60 * 1024 * 1024
WIDTHS = (1152, 384, 1536, 1536)
ROW_BLOCK = 256
UNIT_BLOCK = 512
SMALL_ROWS = 24
NT = (((1,), (1,)), ((), ()))
TN = (((0,), (0,)), ((), ()))
NN = (((1,), (0,)), ((), ()))


def dot(left, right, dims=NN):
    return lax.dot_general(left, right, dims, preferred_element_type=F32)


def gate_values(noise, logit):
    return jax.nn.sigmoid((jnp.log(noise) - jnp.log1p(-noise) + logit) / BETA)


def vmem(n=1):
    return [pl.BlockSpec(memory_space=pltpu.VMEM)] * n


def hbm(n=1):
    return [pl.BlockSpec(memory_space=pl.ANY)] * n


def coords():
    dp = lax.axis_index("dp")
    return dp // 4, lax.rem(dp // 2, 2), lax.axis_index("tensor"), lax.rem(dp, 2)


def place(z, x, y, c):
    return ((z * 2 + x) * 2 + c, y)


def greet():
    z, x, y, c = coords()
    barrier = pltpu.get_barrier_semaphore()
    partners = [(lax.rem(z + k, 4), x, y, c) for k in (1, 2, 3)]
    partners += [(z, 1 - x, y, c), (z, x, 1 - y, c), (z, x, y, 1 - c)]
    for partner in partners:
        pl.semaphore_signal(barrier, inc=1, device_id=place(*partner), device_id_type=MESH)
    pl.semaphore_wait(barrier, len(partners))


class Gather:
    COPIES = 12
    PHASES = 5

    def __init__(self, chunks, ins, outs, local_sem, send_sem, recv_sem):
        self.chunks, self.ins, self.outs = chunks, ins, outs
        self.local_sem, self.send_sem, self.recv_sem = local_sem, send_sem, recv_sem
        self.kept = {}
        self.started = []
        self.locals = []
        self.step_at = 0

    def own(self):
        z, x, y, c = coords()
        for i, (src, dst) in enumerate(zip(self.ins, self.outs)):
            copy = pltpu.make_async_copy(src, dst.at[y, z, x, c], self.local_sem.at[i])
            copy.start()
            self.locals.append(copy)

    def send(self, chunk, slot, src, dst, target):
        copy = pltpu.make_async_remote_copy(
            src_ref=src,
            dst_ref=dst,
            send_sem=self.send_sem.at[chunk, slot],
            recv_sem=self.recv_sem.at[chunk, slot],
            device_id=place(*target),
            device_id_type=MESH,
        )
        copy.start()
        self.started.append(copy)
        self.kept[chunk, slot] = copy

    def arrived(self, chunk, *slots):
        for slot in slots:
            self.kept[chunk, slot].wait_recv()

    def phase(self, chunk, phase):
        z, x, y, c = coords()
        across, beside, core = (z, 1 - x, y, c), (z, x, 1 - y, c), (z, x, y, 1 - c)
        which, start, size = self.chunks[chunk]
        cols = pl.ds(start, size)
        out = self.outs[which]

        def pass_on(slot, view, target):
            self.send(chunk, slot, view, view, target)

        if phase == 0:
            for k in range(3):
                self.send(
                    chunk,
                    k,
                    self.ins[which].at[:, cols],
                    out.at[y, z, x, c, :, cols],
                    (lax.rem(z + k + 1, 4), x, y, c),
                )
        elif phase == 1:
            while self.locals:
                self.locals.pop().wait()
            self.arrived(chunk, 0, 1, 2)
            pass_on(3, out.at[y, 0:2, x, c, :, cols], across)
            pass_on(4, out.at[y, 2:4, x, c, :, cols], beside)
            pass_on(7, out.at[y, :, x, c, :, cols], core)
        elif phase == 2:
            self.arrived(chunk, 3)
            pass_on(5, out.at[y, 0:2, :, c, :, cols], beside)
            self.arrived(chunk, 4)
            pass_on(6, out.at[:, 2:4, x, c, :, cols], across)
            pass_on(8, out.at[y, 0:2, 1 - x, c, :, cols], core)
            pass_on(9, out.at[1 - y, 2:4, x, c, :, cols], core)
        elif phase == 3:
            self.arrived(chunk, 5)
            pass_on(10, out.at[1 - y, 0:2, :, c, :, cols], core)
            self.arrived(chunk, 6)
            pass_on(11, out.at[:, 2:4, 1 - x, c, :, cols], core)
        else:
            self.arrived(chunk, 7, 8, 9, 10, 11)

    def steps(self):
        return len(self.chunks) + self.PHASES - 1

    def step(self):
        if self.step_at < self.steps():
            for phase in range(self.PHASES):
                chunk = self.step_at - phase
                if 0 <= chunk < len(self.chunks):
                    self.phase(chunk, phase)
            self.step_at += 1

    def finish(self):
        while self.step_at < self.steps():
            self.step()
        for copy in self.started:
            copy.wait_send()


def gather_kernel(chunks, count, *refs):
    ins, outs = refs[:count], refs[count : 2 * count]
    gather = Gather(chunks, ins, outs, *refs[2 * count :])
    gather.own()
    greet()
    gather.finish()


def gather_call(chunks, shards):
    count, n = len(shards), len(chunks)
    outs = pl.pallas_call(
        functools.partial(gather_kernel, chunks, count),
        out_shape=[jax.ShapeDtypeStruct((2, 4, 2, 2, 48, s.shape[1]), BF) for s in shards],
        in_specs=hbm(count),
        out_specs=hbm(count),
        scratch_shapes=[
            pltpu.SemaphoreType.DMA((count,)),
            pltpu.SemaphoreType.DMA((n, Gather.COPIES)),
            pltpu.SemaphoreType.DMA((n, Gather.COPIES)),
        ],
        compiler_params=pltpu.CompilerParams(collective_id=1, has_side_effects=True),
        name="gather",
    )(*shards)
    return [o.reshape(2, D, o.shape[-1]) for o in outs]


class Scatter:
    COPIES = 8
    PHASES = 5

    def __init__(self, chunks, grads, outs, bufs, local_sem, send_sem, recv_sem):
        self.chunks, self.grads, self.outs, self.bufs = chunks, grads, outs, bufs
        self.local_sem, self.send_sem, self.recv_sem = local_sem, send_sem, recv_sem
        self.kept = {}
        self.started = []
        self.locals = {}
        self.step_at = 0

    def send(self, chunk, slot, src, dst, target):
        copy = pltpu.make_async_remote_copy(
            src_ref=src,
            dst_ref=dst,
            send_sem=self.send_sem.at[chunk, slot],
            recv_sem=self.recv_sem.at[chunk, slot],
            device_id=place(*target),
            device_id_type=MESH,
        )
        copy.start()
        self.started.append(copy)
        self.kept[chunk, slot] = copy

    def arrived(self, chunk, *slots):
        for slot in slots:
            self.kept[chunk, slot].wait_recv()

    def phase(self, chunk, phase):
        z, x, y, c = coords()
        across, beside, core = (z, 1 - x, y, c), (z, x, 1 - y, c), (z, x, y, 1 - c)
        which, start, size = self.chunks[chunk]
        cols = pl.ds(start, size)
        grad = self.grads[which]
        sums, first, low_a, low_b, next_a, next_b, last_a, last_b, mine, last = self.bufs[chunk]

        def add(dst, left, right):
            dst[...] = (left[...].astype(F32) + right[...].astype(F32)).astype(BF)

        if phase == 0:
            self.send(chunk, 0, grad.at[:, :, :, 1 - c, :, cols], first, core)
            copy = pltpu.make_async_copy(
                grad.at[:, :, :, c, :, cols], sums, self.local_sem.at[chunk]
            )
            copy.start()
            self.locals[chunk] = copy
        elif phase == 1:
            self.locals[chunk].wait()
            self.arrived(chunk, 0)

            @pl.loop(0, 16)
            def _(i):
                at = (i // 8, lax.rem(i // 2, 4), lax.rem(i, 2))
                add(sums.at[at], sums.at[at], first.at[at])

            self.send(chunk, 1, sums.at[1 - y, 0:2], low_a, beside)
            self.send(chunk, 2, sums.at[:, 2:4, 1 - x], low_b, across)
        elif phase == 2:
            self.arrived(chunk, 1)

            @pl.loop(0, 4)
            def _(i):
                at = (i // 2, lax.rem(i, 2))
                add(next_a.at[at], sums.at[(y,) + at], low_a.at[at])

            self.send(chunk, 3, next_a.at[:, 1 - x], last_a, across)
            self.arrived(chunk, 2)

            @pl.loop(0, 4)
            def _(i):
                t, k = i // 2, lax.rem(i, 2)
                add(next_b.at[t, k], sums.at[t, k + 2, x], low_b.at[t, k])

            self.send(chunk, 4, next_b.at[1 - y], last_b, beside)
        elif phase == 3:
            self.arrived(chunk, 3, 4)

            @pl.loop(0, 2)
            def _(k):
                add(mine.at[k], next_a.at[k, x], last_a.at[k])
                add(mine.at[k + 2], next_b.at[y, k], last_b.at[k])

            for k in range(3):
                to = lax.rem(z + k + 1, 4)
                self.send(chunk, 5 + k, mine.at[to], last.at[k], (to, x, y, c))
        else:
            self.arrived(chunk, 5, 6, 7)
            total = mine[z].astype(F32)
            for k in range(3):
                total = total + last[k].astype(F32)
            self.outs[which][:, cols] = total

    def steps(self):
        return len(self.chunks) + self.PHASES - 1

    def step(self):
        if self.step_at < self.steps():
            for phase in range(self.PHASES):
                chunk = self.step_at - phase
                if 0 <= chunk < len(self.chunks):
                    self.phase(chunk, phase)
            self.step_at += 1

    def finish(self):
        while self.step_at < self.steps():
            self.step()
        for copy in self.started:
            copy.wait_send()

    @staticmethod
    def scratch(chunks):
        shapes = []
        for _, _, n in chunks:
            shapes += [
                pltpu.VMEM((2, 4, 2, 48, n), BF),
                pltpu.VMEM((2, 4, 2, 48, n), BF),
                pltpu.VMEM((2, 2, 48, n), BF),
                pltpu.VMEM((2, 2, 48, n), BF),
                pltpu.VMEM((2, 2, 48, n), BF),
                pltpu.VMEM((2, 2, 48, n), BF),
                pltpu.VMEM((2, 48, n), BF),
                pltpu.VMEM((2, 48, n), BF),
                pltpu.VMEM((4, 48, n), BF),
                pltpu.VMEM((3, 48, n), BF),
            ]
        return shapes

    @staticmethod
    def semaphores(chunks):
        n = len(chunks)
        return [
            pltpu.SemaphoreType.DMA((n,)),
            pltpu.SemaphoreType.DMA((n, Scatter.COPIES)),
            pltpu.SemaphoreType.DMA((n, Scatter.COPIES)),
        ]


class Small:
    def __init__(self, out, own, got, lines, send_sem, recv_sem):
        self.out, self.own, self.got, self.lines = out, own, got, lines
        self.send_sem, self.recv_sem = send_sem, recv_sem
        self.pending = []
        self.step_at = 0

    def send(self, slot, src, dst, target):
        copy = pltpu.make_async_remote_copy(
            src_ref=src,
            dst_ref=dst,
            send_sem=self.send_sem.at[slot],
            recv_sem=self.recv_sem.at[slot],
            device_id=place(*target),
            device_id_type=MESH,
        )
        copy.start()
        self.pending.append(copy)

    def step(self):
        z, x, y, c = coords()
        nearby = ((z, x, y, 1 - c), (z, 1 - x, y, c), (z, x, 1 - y, c))
        at = self.step_at
        if at > 4:
            return
        self.step_at += 1
        for copy in self.pending:
            copy.wait()
        self.pending = []
        if 1 <= at <= 3:
            self.own[at] = self.own[at - 1] + self.got[at - 1]
        if at < 3:
            self.send(at, self.own.at[at], self.got.at[at], nearby[at])
        elif at == 3:
            self.lines[z] = self.own[3]
            for k in range(3):
                to = (lax.rem(z + k + 1, 4), x, y, c)
                self.send(3 + k, self.own.at[3], self.lines.at[z], to)
        else:
            self.out[...] = (self.lines[0] + self.lines[1]) + (self.lines[2] + self.lines[3])

    def finish(self):
        while self.step_at <= 4:
            self.step()

    @staticmethod
    def scratch():
        return [
            pltpu.VMEM((4, SMALL_ROWS, D), F32),
            pltpu.VMEM((3, SMALL_ROWS, D), F32),
            pltpu.VMEM((4, SMALL_ROWS, D), F32),
            pltpu.SemaphoreType.DMA((6,)),
            pltpu.SemaphoreType.DMA((6,)),
        ]


def scatter_kernel(chunks, count, *refs):
    grads, small_a, small_b = refs[:count], refs[count], refs[count + 1]
    refs = refs[count + 2 :]
    outs, small_out = refs[:count], refs[count]
    refs = refs[count + 1 :]
    bufs = [refs[10 * i : 10 * i + 10] for i in range(len(chunks))]
    refs = refs[10 * len(chunks) :]
    scatter = Scatter(chunks, grads, outs, bufs, *refs[:3])
    small = Small(small_out, *refs[3:])
    small.own[0] = small_a[...] + small_b[...]
    greet()
    while scatter.step_at < scatter.steps():
        scatter.step()
        small.step()
    small.finish()
    scatter.finish()


def scatter_call(chunks, grads, small_a, small_b):
    count = len(grads)
    grads = [g.reshape(2, 4, 2, 2, 48, g.shape[-1]) for g in grads]
    return pl.pallas_call(
        functools.partial(scatter_kernel, chunks, count),
        out_shape=[jax.ShapeDtypeStruct((48, g.shape[-1]), F32) for g in grads]
        + [jax.ShapeDtypeStruct((SMALL_ROWS, D), F32)],
        in_specs=hbm(count) + vmem(2),
        out_specs=vmem(count + 1),
        scratch_shapes=Scatter.scratch(chunks) + Scatter.semaphores(chunks) + Small.scratch(),
        compiler_params=pltpu.CompilerParams(
            collective_id=2, has_side_effects=True, vmem_limit_bytes=VMEM_BYTES
        ),
        name="scatter",
    )(*grads, small_a, small_b)


def head_masks():
    lane = lax.broadcasted_iota(jnp.int32, (SEQ_LEN, 128), 1)
    return lane < HEAD_DIM


def pair_at(i):
    seq, pair = i // 6, lax.rem(i, 6)
    half, col = pair // 3, lax.rem(pair, 3)
    return seq, half, col, pl.ds(pl.multiple_of(seq * SEQ_LEN, SEQ_LEN), SEQ_LEN)


def lanes(col, base):
    return pl.ds(pl.multiple_of(base + col * 128, 128), 128)


def mask_into(bias, marks_ref, marks_col_ref):
    for s in range(bias.shape[0]):
        same = marks_col_ref[s] == marks_ref[s : s + 1, :]
        bias[s] = jnp.where(same, 0.0, NEG)


def forward_kernel(
    tokens, qkv, out_w, affine, marks, marks_col, mix, context, lse, attn, bias
):
    mask_into(bias, marks, marks_col)
    rows_all = tokens.shape[0]

    @pl.loop(0, rows_all // ROW_BLOCK)
    def _(i):
        rows = pl.ds(pl.multiple_of(i * ROW_BLOCK, ROW_BLOCK), ROW_BLOCK)
        for t in range(2):
            mixed = dot(tokens[rows, :], qkv[t])
            mix[t, rows, :] = ((mixed + affine[t, 0:1, :]) * affine[t, 1:2, :]).astype(BF)

    left = head_masks()

    @pl.loop(0, 12)
    def _(i):
        seq, t, col, rows = pair_at(i)
        query = mix[t, rows, lanes(col, 0)]
        keys = mix[t, rows, lanes(col, 384)]
        values = mix[t, rows, lanes(col, 768)]
        parts = []
        for h in range(2):
            mine = jnp.where(left if h == 0 else ~left, query, 0)
            scores = dot(mine, keys, NT) + bias[seq]
            top = jnp.max(scores, axis=1, keepdims=True)
            expo = jnp.exp(scores - top)
            total = jnp.sum(expo, axis=1, keepdims=True)
            probs = (expo * (1.0 / total)).astype(BF)
            parts.append(dot(probs, values))
            logsum = jnp.broadcast_to(top + jnp.log(total), (SEQ_LEN, 128))
            lse[i, h : h + 1, :] = jnp.transpose(logsum)[0:1, :]
        context[t, rows, lanes(col, 0)] = jnp.where(left, parts[0], parts[1]).astype(BF)

    @pl.loop(0, rows_all // ROW_BLOCK)
    def _(i):
        rows = pl.ds(pl.multiple_of(i * ROW_BLOCK, ROW_BLOCK), ROW_BLOCK)
        attn[rows, :] = dot(context[0, rows, :], out_w[0], NT) + dot(
            context[1, rows, :], out_w[1], NT
        )


def forward_call(tokens, qkv, out_w, affine, marks, marks_col):
    rows = tokens.shape[0]
    seqs = rows // SEQ_LEN
    return pl.pallas_call(
        forward_kernel,
        out_shape=[
            jax.ShapeDtypeStruct((2, rows, 1152), BF),
            jax.ShapeDtypeStruct((2, rows, 384), BF),
            jax.ShapeDtypeStruct((6 * seqs, 8, SEQ_LEN), F32),
            jax.ShapeDtypeStruct((rows, D), F32),
        ],
        in_specs=vmem(6),
        out_specs=vmem(4),
        scratch_shapes=[pltpu.VMEM((seqs, SEQ_LEN, SEQ_LEN), F32)],
        compiler_params=pltpu.CompilerParams(vmem_limit_bytes=VMEM_BYTES),
        name="attention_forward",
    )(tokens, qkv, out_w, affine, marks, marks_col)


def backward_kernel(
    tokens,
    qkv,
    out_w,
    affine,
    marks,
    marks_col,
    mix,
    context,
    lse,
    g_attn,
    g_resid,
    tokens_grad,
    qkv_grad,
    out_grad,
    small,
    bias,
    g_context,
    g_mix,
    tokens_t,
    g_attn_t,
    head_sum,
):
    mask_into(bias, marks, marks_col)
    rows_all = tokens.shape[0]
    head_sum[...] = jnp.zeros_like(head_sum)

    @pl.loop(0, rows_all // ROW_BLOCK)
    def _(i):
        rows = pl.ds(pl.multiple_of(i * ROW_BLOCK, ROW_BLOCK), ROW_BLOCK)
        for t in range(2):
            g_context[t, rows, :] = dot(g_attn[rows, :], out_w[t]).astype(BF)

    for i in range(rows_all // ROW_BLOCK):
        rows = slice(i * ROW_BLOCK, (i + 1) * ROW_BLOCK)
        tokens_t[:, rows] = jnp.transpose(tokens[rows, :])
        g_attn_t[:, rows] = jnp.transpose(g_attn[rows, :])
    for t in range(2):
        out_grad[t] = dot(g_attn_t[...], context[t]).astype(BF)

    left = head_masks()

    @pl.loop(0, 12)
    def _(i):
        seq, t, col, rows = pair_at(i)
        query = mix[t, rows, lanes(col, 0)]
        keys = mix[t, rows, lanes(col, 384)]
        values = mix[t, rows, lanes(col, 768)]
        grad = g_context[t, rows, lanes(col, 0)]
        parts = []
        for h in range(2):
            side = left if h == 0 else ~left
            scores = dot(jnp.where(side, keys, 0), query, NT) + bias[seq]
            probs = jnp.exp(scores - lse[i, h : h + 1, :])
            g_probs = dot(jnp.where(side, values, 0), grad, NT)
            delta = jnp.sum(g_probs * probs, axis=0, keepdims=True)
            g_scores = (probs * (g_probs - delta)).astype(BF)
            parts.append(
                (
                    dot(g_scores, keys, TN),
                    dot(g_scores, query),
                    dot(probs.astype(BF), grad),
                )
            )
        g_query, g_keys, g_values = (jnp.where(left, a, b) for a, b in zip(*parts))
        g_mix[t, rows, lanes(col, 0)] = (g_query * HEAD_DIM**-0.5).astype(BF)
        g_mix[t, rows, lanes(col, 384)] = g_keys.astype(BF)
        v_lanes = lanes(col, 768)
        g_mix[t, rows, v_lanes] = (g_values * affine[t, 1:2, v_lanes]).astype(BF)
        used = jnp.sum(g_values * values.astype(F32), axis=0, keepdims=True)
        head_sum[t, 0:1, lanes(col, 0)] += used

    small[...] = jnp.zeros_like(small)
    ones = jnp.ones((8, rows_all), BF)
    for t in range(2):
        at = slice(384 * t, 384 * (t + 1))
        sums = dot(ones, g_mix[t])
        small[17:18, at] = sums[0:1, 0:384]
        small[18:19, at] = sums[0:1, 768:1152]
        small[19:20, at] = head_sum[t, 0:1, :] / affine[t, 1:2, 768:1152]
        for k in range(3):
            cols = slice(384 * k, 384 * (k + 1))
            qkv_grad[t, :, cols] = dot(tokens_t[...], g_mix[t, :, cols]).astype(BF)

    @pl.loop(0, rows_all // ROW_BLOCK)
    def _(i):
        rows = pl.ds(pl.multiple_of(i * ROW_BLOCK, ROW_BLOCK), ROW_BLOCK)
        tokens_grad[rows, :] = g_resid[rows, :] + (
            dot(g_mix[0, rows, :], qkv[0], NT) + dot(g_mix[1, rows, :], qkv[1], NT)
        )


def backward_call(tokens, qkv, out_w, affine, marks, marks_col, mix, context, lse, g_attn, g_resid):
    rows = tokens.shape[0]
    seqs = rows // SEQ_LEN
    return pl.pallas_call(
        backward_kernel,
        out_shape=[
            jax.ShapeDtypeStruct((rows, D), F32),
            jax.ShapeDtypeStruct((2, D, 1152), BF),
            jax.ShapeDtypeStruct((2, D, 384), BF),
            jax.ShapeDtypeStruct((SMALL_ROWS, D), F32),
        ],
        in_specs=vmem(11),
        out_specs=vmem(4),
        scratch_shapes=[
            pltpu.VMEM((seqs, SEQ_LEN, SEQ_LEN), F32),
            pltpu.VMEM((2, rows, 384), BF),
            pltpu.VMEM((2, rows, 1152), BF),
            pltpu.VMEM((D, rows), BF),
            pltpu.VMEM((D, rows), BF),
            pltpu.VMEM((2, 8, 384), F32),
        ],
        compiler_params=pltpu.CompilerParams(vmem_limit_bytes=VMEM_BYTES),
        name="attention_backward",
    )(tokens, qkv, out_w, affine, marks, marks_col, mix, context, lse, g_attn, g_resid)


def normalise(value):
    mean = jnp.mean(value, axis=1, keepdims=True)
    centred = value - mean
    var = jnp.mean(centred * centred, axis=1, keepdims=True)
    rstd = lax.rsqrt(var + EPS)
    return centred * rstd, rstd


def norm_back(grad, unit, rstd):
    mean = jnp.mean(grad, axis=1, keepdims=True)
    along = jnp.mean(grad * unit, axis=1, keepdims=True)
    return rstd * (grad - mean - unit * along)


def fold(value):
    return jnp.sum(value.reshape(value.shape[0] // 8, 8, value.shape[1]), axis=0)


def feed_kernel(
    tokens,
    teacher,
    attn,
    up_w,
    down_w,
    vec,
    uvec,
    activations,
    g_attn,
    g_resid,
    up_grad,
    down_grad,
    small,
    pre_deriv,
    activ,
    g_pre,
    normed_t,
    g_ffn_t,
    sums,
    unit_sums,
):
    rows_all = tokens.shape[0]
    sums[...] = jnp.zeros_like(sums)
    unit_sums[...] = jnp.zeros_like(unit_sums)
    out_bias, scale1, gain1, shift1 = (vec[i : i + 1, :] for i in range(4))
    down_bias, scale2, gain2, shift2 = (vec[i : i + 1, :] for i in range(4, 8))
    per = 1536 // UNIT_BLOCK

    @pl.loop(0, rows_all // ROW_BLOCK)
    def _(i):
        rows = pl.ds(pl.multiple_of(i * ROW_BLOCK, ROW_BLOCK), ROW_BLOCK)
        attn_b = attn[rows, :] + out_bias
        unit1, rstd1 = normalise(tokens[rows, :].astype(F32) + attn_b * scale1)
        normed = unit1 * gain1 + shift1
        normed_low = normed.astype(BF)
        normed_t[:, rows] = jnp.transpose(normed_low)
        ffn = jnp.zeros((ROW_BLOCK, D), F32)
        for j in range(2 * per):
            t, cols = j // per, slice((j % per) * UNIT_BLOCK, (j % per + 1) * UNIT_BLOCK)
            flat = slice(j * UNIT_BLOCK, (j + 1) * UNIT_BLOCK)
            pre = dot(normed_low, up_w[t, :, cols]) + uvec[0:1, flat]
            gate = uvec[1:2, flat]
            phi = 0.5 + 0.5 * lax.erf(pre * (0.5**0.5))
            pdf = jnp.exp(pre * pre * -0.5) * ((2.0 * jnp.pi) ** -0.5)
            act = (pre * phi * gate).astype(BF)
            pre_deriv[:, flat] = (phi + pre * pdf) * gate
            activ[rows, flat] = act
            ffn = ffn + dot(act, down_w[t, :, cols], NT)
        ffn_b = ffn + down_bias
        unit2, rstd2 = normalise(normed + ffn_b * scale2)
        result = unit2 * gain2 + shift2
        activations[rows, :] = result.astype(BF)
        diff = result - teacher[rows, :].astype(F32)
        g_value2 = norm_back(diff * gain2, unit2, rstd2)
        g_ffn_low = (g_value2 * scale2).astype(BF)
        g_ffn_t[:, rows] = jnp.transpose(g_ffn_low)
        sums[2] += fold(g_value2)
        sums[3] += fold(g_value2 * ffn_b)
        sums[6] += fold(diff * unit2)
        sums[7] += fold(diff)
        sums[8] += fold(diff * diff)
        g_normed = g_value2
        for j in range(2 * per):
            t, cols = j // per, slice((j % per) * UNIT_BLOCK, (j % per + 1) * UNIT_BLOCK)
            flat = slice(j * UNIT_BLOCK, (j + 1) * UNIT_BLOCK)
            g_activ = dot(g_ffn_low, down_w[t, :, cols])
            unit_sums[:, flat] += fold(g_activ * activ[rows, flat].astype(F32))
            grad = (g_activ * pre_deriv[:, flat]).astype(BF)
            g_pre[rows, flat] = grad
            g_normed = g_normed + dot(grad, up_w[t, :, cols], NT)
        g_value1 = norm_back(g_normed * gain1, unit1, rstd1)
        g_resid[rows, :] = g_value1
        g_attn[rows, :] = (g_value1 * scale1).astype(BF)
        sums[0] += fold(g_value1)
        sums[1] += fold(g_value1 * attn_b)
        sums[4] += fold(g_normed * unit1)
        sums[5] += fold(g_normed)

    small[...] = jnp.zeros_like(small)
    for k in range(9):
        small[k : k + 1, :] = jnp.sum(sums[k], axis=0, keepdims=True)
    ones = jnp.ones((8, rows_all), BF)
    for j in range(4):
        cols = slice(768 * j, 768 * (j + 1))
        small[9 + j : 10 + j, :] = dot(ones, g_pre[:, cols])[0:1, :]
        total = jnp.sum(unit_sums[:, cols], axis=0, keepdims=True)
        small[13 + j : 14 + j, :] = total / uvec[1:2, cols]

    @pl.loop(0, FF // UNIT_BLOCK)
    def _(j):
        t = j // per
        flat = pl.ds(pl.multiple_of(j * UNIT_BLOCK, UNIT_BLOCK), UNIT_BLOCK)
        cols = pl.ds(pl.multiple_of(lax.rem(j, per) * UNIT_BLOCK, UNIT_BLOCK), UNIT_BLOCK)
        down_grad[t, :, cols] = dot(g_ffn_t[...], activ[:, flat]).astype(BF)
        up_grad[t, :, cols] = dot(normed_t[...], g_pre[:, flat]).astype(BF)


def feed_call(tokens, teacher, attn, up_w, down_w, vec, uvec):
    rows = tokens.shape[0]
    return pl.pallas_call(
        feed_kernel,
        out_shape=[
            jax.ShapeDtypeStruct((rows, D), BF),
            jax.ShapeDtypeStruct((rows, D), BF),
            jax.ShapeDtypeStruct((rows, D), F32),
            jax.ShapeDtypeStruct((2, D, 1536), BF),
            jax.ShapeDtypeStruct((2, D, 1536), BF),
            jax.ShapeDtypeStruct((SMALL_ROWS, D), F32),
        ],
        in_specs=vmem(7),
        out_specs=vmem(6),
        scratch_shapes=[
            pltpu.VMEM((ROW_BLOCK, FF), F32),
            pltpu.VMEM((rows, FF), BF),
            pltpu.VMEM((rows, FF), BF),
            pltpu.VMEM((D, rows), BF),
            pltpu.VMEM((D, rows), BF),
            pltpu.VMEM((9, 8, D), F32),
            pltpu.VMEM((8, FF), F32),
        ],
        compiler_params=pltpu.CompilerParams(vmem_limit_bytes=VMEM_BYTES),
        name="feed_forward",
    )(tokens, teacher, attn, up_w, down_w, vec, uvec)


GATHER_CHUNKS = (
    (0, 0, 1152),
    (1, 0, 384),
    (2, 0, 768),
    (2, 768, 768),
    (3, 0, 768),
    (3, 768, 768),
)
SCATTER_CHUNKS = (
    (3, 0, 768),
    (3, 768, 768),
    (2, 0, 768),
    (2, 768, 768),
    (1, 0, 384),
    (0, 0, 1152),
)


def body(
    direct,
    tokens,
    teacher,
    segments,
    qkv_weight,
    qkv_bias,
    out_weight,
    out_bias,
    up_weight,
    up_bias,
    down_weight,
    down_bias,
    first_gain,
    first_shift,
    second_gain,
    second_shift,
    head_logit,
    unit_logit,
    width_logit,
    layer_logit,
    head_noise,
    unit_noise,
    width_noise,
    layer_noise,
):
    z_head = gate_values(head_noise, head_logit)
    z_unit = gate_values(unit_noise, unit_logit)
    z_width = gate_values(width_noise, width_logit)
    z_layer = gate_values(layer_noise, layer_logit)
    shards = (qkv_weight.reshape(-1, 1152), out_weight, up_weight, down_weight)
    if direct:
        full = gather_call(GATHER_CHUNKS, shards)
    else:
        full = [
            lax.all_gather(lax.all_gather(s, "dp", axis=0, tiled=True), "tensor", axis=0)
            for s in shards
        ]
    qkv_full, out_full, up_full, down_full = full
    by_half = lambda v: v.reshape(2, 384)
    zh = by_half(jnp.repeat(z_head, HEAD_DIM))
    zeros, ones = jnp.zeros((2, 384), F32), jnp.ones((2, 384), F32)
    affine = jnp.stack(
        [
            jnp.concatenate([by_half(qkv_bias[0]), zeros, by_half(qkv_bias[1])], axis=1),
            jnp.concatenate([ones * HEAD_DIM**-0.5, ones, zh], axis=1),
        ],
        axis=1,
    )
    scale1, scale2 = z_layer[0] * z_width, z_layer[1] * z_width
    vec = jnp.stack(
        [
            out_bias,
            scale1,
            first_gain,
            first_shift,
            down_bias,
            scale2,
            second_gain,
            second_shift,
        ]
    )
    uvec = jnp.stack([up_bias, z_unit])
    marks, marks_col = segments, segments[:, :, None]
    mix, context, lse, attn = forward_call(tokens, qkv_full, out_full, affine, marks, marks_col)
    activations, g_attn, g_resid, up_grad, down_grad, small_a = feed_call(
        tokens, teacher, attn, up_full, down_full, vec, uvec
    )
    tokens_grad, qkv_grad, out_grad, small_b = backward_call(
        tokens, qkv_full, out_full, affine, marks, marks_col, mix, context, lse, g_attn, g_resid
    )
    grads = (qkv_grad, out_grad, up_grad, down_grad)
    if direct:
        *grads, small = scatter_call(SCATTER_CHUNKS, grads, small_a, small_b)
    else:
        grads = [
            lax.psum_scatter(
                lax.psum_scatter(g, "tensor", scatter_dimension=0),
                "dp",
                scatter_dimension=0,
                tiled=True,
            ).astype(F32)
            for g in grads
        ]
        small = lax.psum(small_a + small_b, ("dp", "tensor"))
    qkv_grad, out_grad, up_grad, down_grad = grads
    slope = lambda gate: gate * (1.0 - gate) * 1.5
    all_tokens = tokens.shape[0] * lax.axis_size("dp") * lax.axis_size("tensor")
    width_grad = (small[1] * z_layer[0] + small[3] * z_layer[1]) * slope(z_width)
    layer_grad = jnp.stack([jnp.sum(small[1] * z_width), jnp.sum(small[3] * z_width)])
    return (
        activations,
        0.5 * jnp.sum(small[8]) / all_tokens,
        tokens_grad,
        qkv_grad.reshape(-1, 3, 384),
        small[17:19],
        out_grad,
        small[0] * scale1,
        up_grad,
        small[9:13].reshape(FF),
        down_grad,
        small[2] * scale2,
        small[4],
        small[5],
        small[6],
        small[7],
        jnp.sum(small[19].reshape(HEADS, HEAD_DIM), axis=1) * slope(z_head),
        small[13:17].reshape(FF) * slope(z_unit),
        width_grad,
        layer_grad * slope(z_layer),
    )


def solution(mesh):
    rows, split, whole = P(("dp", "tensor"), None), P("dp", "tensor"), P()
    cube = P("dp", None, "tensor")
    in_specs = (rows, rows, rows, cube, whole, split, whole, split, whole, split) + (whole,) * 13
    out_specs = (
        rows,
        whole,
        rows,
        cube,
        whole,
        split,
        whole,
        split,
        whole,
        split,
    ) + (whole,) * 9
    direct = mesh.shape["dp"] == 16 and mesh.shape["tensor"] == 2
    return jax.shard_map(
        functools.partial(body, direct),
        mesh=mesh,
        in_specs=in_specs,
        out_specs=out_specs,
        check_vma=False,
    )
```

```python
import functools

import jax
import jax.numpy as jnp
from jax import lax
from jax.experimental import pallas as pl
from jax.experimental.pallas import tpu as pltpu
from jax.sharding import PartitionSpec as P

D = 768
HEADS = 12
HEAD_DIM = 64
FF = 3072
SEQ_LEN = 512
BETA = 2.0 / 3.0
EPS = 1e-12
NEG = -1e30
BF = jnp.bfloat16
F32 = jnp.float32
MESH = pl.DeviceIdType.MESH
VMEM_BYTES = 60 * 1024 * 1024
WIDTHS = (1152, 384, 1536, 1536)
ROW_BLOCK = 256
SMALL_ROWS = 24
NT = (((1,), (1,)), ((), ()))
TN = (((0,), (0,)), ((), ()))
NN = (((1,), (0,)), ((), ()))


def dot(left, right, dims=NN):
    return lax.dot_general(left, right, dims, preferred_element_type=F32)


def vmem(n=1):
    return [pl.BlockSpec(memory_space=pltpu.VMEM)] * n


def hbm(n=1):
    return [pl.BlockSpec(memory_space=pl.ANY)] * n


def coords():
    dp = lax.axis_index("dp")
    return dp // 4, lax.rem(dp // 2, 2), lax.axis_index("tensor"), lax.rem(dp, 2)


def place(z, x, y, c):
    return ((z * 2 + x) * 2 + c, y)


def partners():
    z, x, y, c = coords()
    along = [(lax.rem(z + k, 4), x, y, c) for k in (1, 2, 3)]
    return along + [(z, 1 - x, y, c), (z, x, 1 - y, c), (z, x, y, 1 - c)]


def greet():
    barrier = pltpu.get_barrier_semaphore()
    for partner in partners():
        pl.semaphore_signal(barrier, inc=1, device_id=place(*partner), device_id_type=MESH)


def met():
    pl.semaphore_wait(pltpu.get_barrier_semaphore(), 6)


class Gather:
    COPIES = 12

    def __init__(self, chunks, ins, outs, local_sem, send_sem, recv_sem):
        self.chunks, self.ins, self.outs = chunks, ins, outs
        self.local_sem, self.send_sem, self.recv_sem = local_sem, send_sem, recv_sem
        self.kept = {}
        self.started = []
        self.locals = {}

    def send(self, chunk, slot, src, dst, target):
        copy = pltpu.make_async_remote_copy(
            src_ref=src,
            dst_ref=dst,
            send_sem=self.send_sem.at[chunk, slot],
            recv_sem=self.recv_sem.at[chunk, slot],
            device_id=place(*target),
            device_id_type=MESH,
        )
        copy.start()
        self.started.append(copy)
        self.kept[chunk, slot] = copy

    def arrived(self, chunk, *slots):
        for slot in slots:
            self.kept[chunk, slot].wait_recv()

    def source(self, chunk):
        which, start, size = self.chunks[chunk]
        if which == 0:
            return self.ins[0].at[start // size]
        return self.ins[which].at[:, pl.ds(start, size)]

    def target(self, chunk):
        which, start, size = self.chunks[chunk]
        z, x, y, c = coords()
        return self.outs[which].at[y, z, x, c, :, pl.ds(start, size)]

    def own(self):
        for i in range(len(self.chunks)):
            copy = pltpu.make_async_copy(self.source(i), self.target(i), self.local_sem.at[i])
            copy.start()
            self.locals[i] = copy

    def phase(self, chunk, phase):
        z, x, y, c = coords()
        across, beside, core = (z, 1 - x, y, c), (z, x, 1 - y, c), (z, x, y, 1 - c)
        which, start, size = self.chunks[chunk]
        cols = pl.ds(start, size)
        out = self.outs[which]

        def pass_on(slot, view, target):
            self.send(chunk, slot, view, view, target)

        if phase == 0:
            for k in range(3):
                self.send(
                    chunk,
                    k,
                    self.source(chunk),
                    self.target(chunk),
                    (lax.rem(z + k + 1, 4), x, y, c),
                )
        elif phase == 1:
            self.locals[chunk].wait()
            self.arrived(chunk, 0, 1, 2)
            pass_on(3, out.at[y, 0:2, x, c, :, cols], across)
            pass_on(4, out.at[y, 2:4, x, c, :, cols], beside)
            pass_on(7, out.at[y, :, x, c, :, cols], core)
        elif phase == 2:
            self.arrived(chunk, 3)
            pass_on(5, out.at[y, 0:2, :, c, :, cols], beside)
            self.arrived(chunk, 4)
            pass_on(6, out.at[:, 2:4, x, c, :, cols], across)
            pass_on(8, out.at[y, 0:2, 1 - x, c, :, cols], core)
            pass_on(9, out.at[1 - y, 2:4, x, c, :, cols], core)
        elif phase == 3:
            self.arrived(chunk, 5)
            pass_on(10, out.at[1 - y, 0:2, :, c, :, cols], core)
            self.arrived(chunk, 6)
            pass_on(11, out.at[:, 2:4, 1 - x, c, :, cols], core)
        else:
            self.arrived(chunk, 7, 8, 9, 10, 11)

    def finish(self):
        for copy in self.started:
            copy.wait_send()


class Scatter:
    COPIES = 8

    def __init__(self, chunks, outs, bufs, send_sem, recv_sem):
        self.chunks, self.outs, self.bufs = chunks, outs, bufs
        self.send_sem, self.recv_sem = send_sem, recv_sem
        self.kept = {}
        self.started = {}

    def send(self, chunk, slot, src, dst, target):
        copy = pltpu.make_async_remote_copy(
            src_ref=src,
            dst_ref=dst,
            send_sem=self.send_sem.at[chunk, slot],
            recv_sem=self.recv_sem.at[chunk, slot],
            device_id=place(*target),
            device_id_type=MESH,
        )
        copy.start()
        self.started.setdefault(chunk, []).append(copy)
        self.kept[chunk, slot] = copy

    def arrived(self, chunk, *slots):
        for slot in slots:
            self.kept[chunk, slot].wait_recv()

    def release(self, chunk):
        for copy in self.started.pop(chunk, []):
            copy.wait_send()

    def views(self, chunk):
        _, _, size, at, lane = self.chunks[chunk]
        return tuple(
            ref.at[(slice(None),) * (len(ref.shape) - 1) + (pl.ds(lane, size),)]
            for ref in self.bufs[at]
        )

    def fill(self, chunk, half, value):
        c = coords()[3]
        both = self.views(chunk)[0]
        for i in range(16):
            z, x, k = i // 4, (i // 2) % 2, i % 2
            side = lax.rem(c + k, 2)
            both[side, half, z, x] = value[48 * i : 48 * (i + 1), :].astype(BF)

    def phase(self, chunk, phase):
        z, x, y, c = coords()
        across, beside, core = (z, 1 - x, y, c), (z, x, 1 - y, c), (z, x, y, 1 - c)
        both, first, low_a, low_b, last_a, last_b, last = self.views(chunk)
        sums = both.at[0]

        def add(left, right):
            left[...] = (left[...].astype(F32) + right[...].astype(F32)).astype(BF)

        if phase == 0:
            self.send(chunk, 0, both.at[1], first, core)
        elif phase == 1:
            self.arrived(chunk, 0)

            @pl.loop(0, 16)
            def _(i):
                at = (i // 8, lax.rem(i // 2, 4), lax.rem(i, 2))
                add(sums.at[at], first.at[at])

            self.send(chunk, 1, sums.at[1 - y, 0:2], low_a, beside)
            self.send(chunk, 2, sums.at[:, 2:4, 1 - x], low_b, across)
        elif phase == 2:
            self.arrived(chunk, 1)

            @pl.loop(0, 4)
            def _(i):
                k, v = i // 2, lax.rem(i, 2)
                add(sums.at[y, k, v], low_a.at[k, v])

            self.send(chunk, 3, sums.at[y, 0:2, 1 - x], last_a, across)
            self.arrived(chunk, 2)

            @pl.loop(0, 4)
            def _(i):
                t, k = i // 2, lax.rem(i, 2)
                add(sums.at[t, k + 2, x], low_b.at[t, k])

            self.send(chunk, 4, sums.at[1 - y, 2:4, x], last_b, beside)
        elif phase == 3:
            self.arrived(chunk, 3, 4)

            @pl.loop(0, 2)
            def _(k):
                add(sums.at[y, k, x], last_a.at[k])
                add(sums.at[y, k + 2, x], last_b.at[k])

            for k in range(3):
                to = lax.rem(z + k + 1, 4)
                self.send(chunk, 5 + k, sums.at[y, to, x], last.at[k], (to, x, y, c))
        else:
            self.arrived(chunk, 5, 6, 7)
            total = sums[y, z, x].astype(F32)
            for k in range(3):
                total = total + last[k].astype(F32)
            which, start, size = self.chunks[chunk][:3]
            if which == 0:
                for kind in range(3):
                    part = total[:, 128 * kind : 128 * (kind + 1)]
                    self.outs[0][kind, :, pl.ds(start, 128)] = part
            else:
                self.outs[which][:, pl.ds(start, size)] = total

    def finish(self):
        for chunk in list(self.started):
            self.release(chunk)

    @staticmethod
    def scratch(sizes):
        shapes = []
        for n in sizes:
            shapes += [
                pltpu.VMEM((2, 2, 4, 2, 48, n), BF),
                pltpu.VMEM((2, 4, 2, 48, n), BF),
                pltpu.VMEM((2, 2, 48, n), BF),
                pltpu.VMEM((2, 2, 48, n), BF),
                pltpu.VMEM((2, 48, n), BF),
                pltpu.VMEM((2, 48, n), BF),
                pltpu.VMEM((3, 48, n), BF),
            ]
        return shapes

    @staticmethod
    def semaphores(chunks):
        n = len(chunks)
        return [
            pltpu.SemaphoreType.DMA((n, Scatter.COPIES)),
            pltpu.SemaphoreType.DMA((n, Scatter.COPIES)),
        ]


class Small:
    def __init__(self, out, own, got, lines, send_sem, recv_sem):
        self.out, self.own, self.got, self.lines = out, own, got, lines
        self.send_sem, self.recv_sem = send_sem, recv_sem
        self.pending = []
        self.step_at = 0

    def send(self, slot, src, dst, target):
        copy = pltpu.make_async_remote_copy(
            src_ref=src,
            dst_ref=dst,
            send_sem=self.send_sem.at[slot],
            recv_sem=self.recv_sem.at[slot],
            device_id=place(*target),
            device_id_type=MESH,
        )
        copy.start()
        self.pending.append(copy)

    def step(self):
        z, x, y, c = coords()
        nearby = ((z, x, y, 1 - c), (z, 1 - x, y, c), (z, x, 1 - y, c))
        at = self.step_at
        if at > 4:
            return
        self.step_at += 1
        for copy in self.pending:
            copy.wait()
        self.pending = []
        if 1 <= at <= 3:
            self.own[at] = self.own[at - 1] + self.got[at - 1]
        if at < 3:
            self.send(at, self.own.at[at], self.got.at[at], nearby[at])
        elif at == 3:
            self.lines[z] = self.own[3]
            for k in range(3):
                to = (lax.rem(z + k + 1, 4), x, y, c)
                self.send(3 + k, self.own.at[3], self.lines.at[z], to)
        else:
            self.out[...] = (self.lines[0] + self.lines[1]) + (self.lines[2] + self.lines[3])

    def finish(self):
        while self.step_at <= 4:
            self.step()

    @staticmethod
    def scratch():
        return [
            pltpu.VMEM((4, SMALL_ROWS, D), F32),
            pltpu.VMEM((3, SMALL_ROWS, D), F32),
            pltpu.VMEM((4, SMALL_ROWS, D), F32),
            pltpu.SemaphoreType.DMA((6,)),
            pltpu.SemaphoreType.DMA((6,)),
        ]


def head_masks():
    lane = lax.broadcasted_iota(jnp.int32, (SEQ_LEN, 128), 1)
    return lane < HEAD_DIM


def pair_at(i):
    seq, pair = i // 6, lax.rem(i, 6)
    half, col = pair // 3, lax.rem(pair, 3)
    return seq, half, col, pl.ds(pl.multiple_of(seq * SEQ_LEN, SEQ_LEN), SEQ_LEN)


def lanes(col, base):
    return pl.ds(pl.multiple_of(base + col * 128, 128), 128)


def mask_into(bias, marks):
    for s in range(bias.shape[0]):
        item = lax.broadcasted_iota(jnp.int32, (16, SEQ_LEN), 0)
        hot = jnp.where(marks[s : s + 1, :] == item, 1.0, 0.0).astype(BF)
        bias[s] = (dot(hot, hot, TN) - 1.0) * -NEG


def gate(noise, logit):
    return jax.nn.sigmoid((jnp.log(noise) - jnp.log1p(-noise) + logit) * (1.0 / BETA))


def flat_row(ref):
    return ref[...].reshape(1, ref.shape[0])


def over_heads(values):
    head = lax.broadcasted_iota(jnp.int32, (1, D), 1) // HEAD_DIM
    out = jnp.zeros((1, D), F32)
    for h in range(HEADS):
        out = jnp.where(head == h, values[:, h : h + 1], out)
    return out


def prepare(raw, affine, vec, uvec):
    zh = over_heads(gate_of(raw, HEAD))
    zw = gate_of(raw, WIDTH)
    zl = gate_of(raw, LAYER)
    for t in range(2):
        cols = slice(384 * t, 384 * (t + 1))
        affine[t, 0:1, 0:384] = raw[QKV_BIAS][0:1, cols]
        affine[t, 0:1, 384:768] = jnp.zeros((1, 384), F32)
        affine[t, 0:1, 768:1152] = raw[QKV_BIAS][1:2, cols]
        affine[t, 1:2, 0:384] = jnp.full((1, 384), HEAD_DIM**-0.5, F32)
        affine[t, 1:2, 384:768] = jnp.ones((1, 384), F32)
        affine[t, 1:2, 768:1152] = zh[:, cols]
    for i, name in enumerate(VEC):
        vec[i : i + 1, :] = zl[:, i // 4 : i // 4 + 1] * zw if name is None else flat_row(raw[name])
    uvec[0:1, :] = flat_row(raw[UP_BIAS])
    uvec[1:2, :] = gate_of(raw, UNIT)


QKV_BIAS, OUT_BIAS, UP_BIAS, DOWN_BIAS, GAIN1, SHIFT1, GAIN2, SHIFT2 = range(8)
LOGITS, NOISES = 8, 12
HEAD, UNIT, WIDTH, LAYER = range(4)
PREP = 16
VEC = (OUT_BIAS, None, GAIN1, SHIFT1, DOWN_BIAS, None, GAIN2, SHIFT2)


def gate_of(raw, kind):
    return gate(flat_row(raw[NOISES + kind]), flat_row(raw[LOGITS + kind]))


def project(i, tokens, weight, affine, mix):
    rows = pl.ds(pl.multiple_of(i * ROW_BLOCK, ROW_BLOCK), ROW_BLOCK)
    for t in range(2):
        mixed = dot(tokens[rows, :], weight(t))
        mix[t, rows, :] = ((mixed + affine[t, 0:1, :]) * affine[t, 1:2, :]).astype(BF)


def attend(i, mix, bias, context, lse):
    left = head_masks()
    seq, t, col, rows = pair_at(i)
    query = mix[t, rows, lanes(col, 0)]
    keys = mix[t, rows, lanes(col, 384)]
    values = mix[t, rows, lanes(col, 768)]
    parts = []
    for h in range(2):
        mine = jnp.where(left if h == 0 else ~left, query, 0)
        scores = dot(mine, keys, NT) + bias[seq]
        top = jnp.max(scores, axis=1, keepdims=True)
        expo = jnp.exp(scores - top)
        total = jnp.sum(expo, axis=1, keepdims=True)
        probs = (expo * (1.0 / total)).astype(BF)
        parts.append(dot(probs, values))
        logsum = jnp.broadcast_to(top + jnp.log(total), (SEQ_LEN, 128))
        lse[i, h : h + 1, :] = jnp.transpose(logsum)[0:1, :]
    context[t, rows, lanes(col, 0)] = jnp.where(left, parts[0], parts[1]).astype(BF)


def attend_back(m, mix, bias, lse, g_context, affine, g_mix, head_sum):
    left = head_masks()
    seq, t, col = lax.rem(m, 2), lax.rem(m // 2, 2), m // 4
    i = seq * 6 + t * 3 + col
    rows = pl.ds(pl.multiple_of(seq * SEQ_LEN, SEQ_LEN), SEQ_LEN)
    query = mix[t, rows, lanes(col, 0)]
    keys = mix[t, rows, lanes(col, 384)]
    values = mix[t, rows, lanes(col, 768)]
    grad = g_context[t, rows, lanes(col, 0)]
    parts = []
    for h in range(2):
        side = left if h == 0 else ~left
        scores = dot(jnp.where(side, keys, 0), query, NT) + bias[seq]
        probs = jnp.exp(scores - lse[i, h : h + 1, :])
        g_probs = dot(jnp.where(side, values, 0), grad, NT)
        delta = jnp.sum(g_probs * probs, axis=0, keepdims=True)
        g_scores = (probs * (g_probs - delta)).astype(BF)
        parts.append(
            (
                dot(g_scores, keys, TN),
                dot(g_scores, query),
                dot(probs.astype(BF), grad),
            )
        )
    g_query, g_keys, g_values = (jnp.where(left, a, b) for a, b in zip(*parts))
    g_mix[t, rows, lanes(3 * col, 0)] = (g_query * HEAD_DIM**-0.5).astype(BF)
    g_mix[t, rows, lanes(3 * col, 128)] = g_keys.astype(BF)
    used = affine[t, 1:2, lanes(col, 768)]
    g_mix[t, rows, lanes(3 * col, 256)] = (g_values * used).astype(BF)
    used = jnp.sum(g_values * values.astype(F32), axis=0, keepdims=True)
    head_sum[t, 0:1, lanes(col, 0)] += used


def normalise(value):
    mean = jnp.mean(value, axis=1, keepdims=True)
    centred = value - mean
    var = jnp.mean(centred * centred, axis=1, keepdims=True)
    rstd = lax.rsqrt(var + EPS)
    return centred * rstd, rstd


def norm_back(grad, unit, rstd):
    mean = jnp.mean(grad, axis=1, keepdims=True)
    along = jnp.mean(grad * unit, axis=1, keepdims=True)
    return rstd * (grad - mean - unit * along)


def fold(value):
    return jnp.sum(value.reshape(value.shape[0] // 8, 8, value.shape[1]), axis=0)


START, PROJECT, PAIRS, UP = range(4)
ARRIVE = {
    (START, 0): (
        ((0, 0), (1, 0), (2, 0), (0, 1), (3, 0), (1, 1), (0, 2), (4, 0), (2, 1), (1, 2), (0, 3))
        + ((5, 0), (3, 1), (2, 2), (1, 3), (6, 0), (4, 1), (3, 2), (2, 3), (0, 4), (1, 4), (2, 4))
    ),
    (PROJECT, 0): ((7, 0), (5, 1), (4, 2)),
    (PROJECT, 1): ((3, 3),),
    (PAIRS, 0): ((6, 1), (5, 2)),
    (PAIRS, 1): ((7, 1), (4, 3), (3, 4)),
    (PAIRS, 2): ((6, 2),),
    (PAIRS, 3): ((5, 3), (4, 4), (5, 4)),
    (UP, 0): ((7, 2),),
    (UP, 1): ((6, 3),),
    (UP, 2): ((7, 3), (6, 4), (7, 4)),
}


def forward_kernel(direct, *refs):
    tokens, teacher, marks = refs[:3]
    raw = refs[3 : 3 + PREP]
    refs = refs[3 + PREP :]
    weights, refs = refs[:4], refs[4:]
    if direct:
        full, refs = refs[:2], refs[2:]
    lse, affine, vec, small = refs[:4]
    out = refs[4 : 4 + STREAMED]
    refs = refs[4 + STREAMED :]
    held, refs = refs[:4], refs[4:]
    mix, context, attn, bias, uvec, deriv, activ = refs[:7]
    normed_t, g_ffn_t, result_low, g_attn, sums, unit_sums = refs[7:13]
    keep_sem, load_sem, stream_sem = refs[13:16]
    refs = refs[16:]
    rows_all = tokens.shape[0]
    blocks = rows_all // ROW_BLOCK
    if direct:
        gather = Gather(GATHER_CHUNKS, weights, held, *refs)
        greet()
        gather.own()
        prepare(raw, affine, vec, uvec)
        met()
    else:
        loads = [pltpu.make_async_copy(*pair, load_sem.at[i]) for i, pair in enumerate(zip(weights, held))]
        for copy in loads:
            copy.start()
        prepare(raw, affine, vec, uvec)
        for copy in loads:
            copy.wait()
    mask_into(bias, marks)
    sums[...] = jnp.zeros_like(sums)
    unit_sums[...] = jnp.zeros_like(unit_sums)

    def weight(which, t):
        return held[which][t].reshape(D, WIDTHS[which])

    def comm(piece, i=0):
        if direct:
            for chunk, phase in ARRIVE.get((piece, i), ()):
                gather.phase(chunk, phase)

    kept = []

    def keep(src, dst):
        copy = pltpu.make_async_copy(src, dst, keep_sem.at[len(kept)])
        copy.start()
        kept.append(copy)

    def row_span(i):
        start = i * ROW_BLOCK
        return pl.ds(start if isinstance(i, int) else pl.multiple_of(start, ROW_BLOCK), ROW_BLOCK)

    def stream(name, i):
        rows = row_span(i)
        across = out[name].at[:, rows] if name in (NORMED_T, G_FFN_T) else out[name].at[rows]
        source = {
            ACTIVATIONS: result_low,
            G_ATTN: g_attn,
            G_RESID: attn,
            ACTIV: activ,
            G_PRE: activ,
        }
        if name in source:
            src = source[name].at[rows]
        else:
            src = (normed_t if name == NORMED_T else g_ffn_t).at[i]
        return pltpu.make_async_copy(src, across, stream_sem.at[name, i])

    comm(START)
    if direct:
        keep(held[0], full[0])
    for half in range(2):

        @pl.loop(0, blocks // 2)
        def _(i):
            project(half * (blocks // 2) + i, tokens, lambda t: weight(0, t), affine, mix)

        comm(PROJECT, half)
    for part in range(4):

        @pl.loop(3 * part, 3 * part + 3)
        def _(i):
            attend(i, mix, bias, context, lse)

        comm(PAIRS, part)
    if direct:
        keep(held[1], full[1])
    keep(mix, out[MIX])
    keep(context, out[CONTEXTS])
    out_bias, scale1, gain1, shift1 = (vec[i : i + 1, :] for i in range(4))
    down_bias, scale2, gain2, shift2 = (vec[i : i + 1, :] for i in range(4, 8))

    def upward(i):
        rows = row_span(i)
        both = dot(context[0, rows, :], weight(1, 0), NT) + dot(context[1, rows, :], weight(1, 1), NT)
        attn[rows, :] = both
        unit1, _ = normalise(tokens[rows, :].astype(F32) + (both + out_bias) * scale1)
        normed_low = (unit1 * gain1 + shift1).astype(BF)
        normed_t[i] = jnp.transpose(normed_low)
        stream(NORMED_T, i).start()
        for t in range(2):
            flat = slice(1536 * t, 1536 * (t + 1))
            pre = dot(normed_low, weight(2, t)) + uvec[0:1, flat]
            gates = uvec[1:2, flat]
            phi = 0.5 + 0.5 * lax.erf(pre * (0.5**0.5))
            pdf = jnp.exp(pre * pre * -0.5) * ((2.0 * jnp.pi) ** -0.5)
            deriv[rows, flat] = (phi + pre * pdf) * gates
            activ[rows, flat] = (pre * phi * gates).astype(BF)
        stream(ACTIV, i).start()

    upward(0)
    comm(UP, 0)
    upward(1)
    comm(UP, 1)

    @pl.loop(2, blocks)
    def _(i):
        upward(i)

    comm(UP, 2)

    @pl.loop(0, blocks)
    def _(i):
        rows = row_span(i)
        attn_b = attn[rows, :] + out_bias
        unit1, rstd1 = normalise(tokens[rows, :].astype(F32) + attn_b * scale1)
        normed = unit1 * gain1 + shift1
        ffn_b = (
            dot(activ[rows, 0:1536], weight(3, 0), NT) + dot(activ[rows, 1536:3072], weight(3, 1), NT)
        ) + down_bias
        unit2, rstd2 = normalise(normed + ffn_b * scale2)
        result = unit2 * gain2 + shift2
        result_low[rows, :] = result.astype(BF)
        stream(ACTIVATIONS, i).start()
        diff = result - teacher[rows, :].astype(F32)
        g_value2 = norm_back(diff * gain2, unit2, rstd2)
        g_ffn_low = (g_value2 * scale2).astype(BF)
        g_ffn_t[i] = jnp.transpose(g_ffn_low)
        stream(G_FFN_T, i).start()
        sums[2] += fold(g_value2)
        sums[3] += fold(g_value2 * ffn_b)
        sums[6] += fold(diff * unit2)
        sums[7] += fold(diff)
        sums[8] += fold(diff * diff)
        ones = jnp.ones((8, ROW_BLOCK), BF)
        stream(ACTIV, i).wait()
        g_normed = g_value2
        for t in range(2):
            flat = slice(1536 * t, 1536 * (t + 1))
            g_activ = dot(g_ffn_low, weight(3, t))
            unit_sums[0, :, flat] += fold(g_activ * activ[rows, flat].astype(F32))
            grad = (g_activ * deriv[rows, flat]).astype(BF)
            activ[rows, flat] = grad
            unit_sums[1, :, flat] += dot(ones, grad)
            g_normed = g_normed + dot(grad, weight(2, t), NT)
        stream(G_PRE, i).start()
        g_value1 = norm_back(g_normed * gain1, unit1, rstd1)
        attn[rows, :] = g_value1
        stream(G_RESID, i).start()
        g_attn[rows, :] = (g_value1 * scale1).astype(BF)
        stream(G_ATTN, i).start()
        sums[0] += fold(g_value1)
        sums[1] += fold(g_value1 * attn_b)
        sums[4] += fold(g_normed * unit1)
        sums[5] += fold(g_normed)

    small[...] = jnp.zeros_like(small)
    for k in range(9):
        small[k : k + 1, :] = jnp.sum(sums[k], axis=0, keepdims=True)
    for j in range(4):
        cols = slice(768 * j, 768 * (j + 1))
        small[9 + j : 10 + j, :] = unit_sums[1, 0:1, cols]
        total = jnp.sum(unit_sums[0, :, cols], axis=0, keepdims=True)
        small[13 + j : 14 + j, :] = total / uvec[1:2, cols]
    for name in range(2, STREAMED):
        for i in range(blocks):
            if name != ACTIV:
                stream(name, i).wait()
    for copy in kept:
        copy.wait()
    if direct:
        gather.finish()


MIX, CONTEXTS, ACTIVATIONS, G_ATTN, G_RESID, ACTIV, G_PRE, NORMED_T, G_FFN_T = range(9)
STREAMED = 9
QKV_W, OUT_W, TOKENS = range(9, 12)


def forward_call(direct, tokens, teacher, marks, raw, weights):
    rows = tokens.shape[0]
    seqs = rows // SEQ_LEN
    blocks = rows // ROW_BLOCK
    n = len(GATHER_CHUNKS)
    full = [jax.ShapeDtypeStruct((2, 4, 2, 2, 48, w), BF) for w in WIDTHS]
    shapes = [
        jax.ShapeDtypeStruct((6 * seqs, 8, SEQ_LEN), F32),
        jax.ShapeDtypeStruct((2, 8, 1152), F32),
        jax.ShapeDtypeStruct((8, D), F32),
        jax.ShapeDtypeStruct((SMALL_ROWS, D), F32),
    ]
    streamed = [
        jax.ShapeDtypeStruct((2, rows, 1152), BF),
        jax.ShapeDtypeStruct((2, rows, 384), BF),
        jax.ShapeDtypeStruct((rows, D), BF),
        jax.ShapeDtypeStruct((rows, D), BF),
        jax.ShapeDtypeStruct((rows, D), F32),
        jax.ShapeDtypeStruct((rows, FF), BF),
        jax.ShapeDtypeStruct((rows, FF), BF),
        jax.ShapeDtypeStruct((D, rows), BF),
        jax.ShapeDtypeStruct((D, rows), BF),
    ]
    scratch = [pltpu.VMEM(f.shape, BF) for f in full]
    scratch += [
        pltpu.VMEM((2, rows, 1152), BF),
        pltpu.VMEM((2, rows, 384), BF),
        pltpu.VMEM((rows, D), F32),
        pltpu.VMEM((seqs, SEQ_LEN, SEQ_LEN), F32),
        pltpu.VMEM((8, FF), F32),
        pltpu.VMEM((rows, FF), F32),
        pltpu.VMEM((rows, FF), BF),
        pltpu.VMEM((blocks, D, ROW_BLOCK), BF),
        pltpu.VMEM((blocks, D, ROW_BLOCK), BF),
        pltpu.VMEM((rows, D), BF),
        pltpu.VMEM((rows, D), BF),
        pltpu.VMEM((9, 8, D), F32),
        pltpu.VMEM((2, 8, FF), F32),
        pltpu.SemaphoreType.DMA((4,)),
        pltpu.SemaphoreType.DMA((4,)),
        pltpu.SemaphoreType.DMA((STREAMED, blocks)),
    ]
    extra = {}
    if direct:
        scratch += [
            pltpu.SemaphoreType.DMA((n,)),
            pltpu.SemaphoreType.DMA((n, Gather.COPIES)),
            pltpu.SemaphoreType.DMA((n, Gather.COPIES)),
        ]
        extra = dict(collective_id=1, has_side_effects=True)
    else:
        weights = [w.reshape(f.shape) for w, f in zip(weights, full)]
    outs = pl.pallas_call(
        functools.partial(forward_kernel, direct),
        out_shape=(full[:2] if direct else []) + shapes + streamed,
        in_specs=vmem(3 + PREP) + (vmem(4) if direct else hbm(4)),
        out_specs=(hbm(2) if direct else []) + vmem(len(shapes)) + hbm(len(streamed)),
        scratch_shapes=scratch,
        compiler_params=pltpu.CompilerParams(vmem_limit_bytes=VMEM_BYTES, **extra),
        name="forward",
    )(tokens, teacher, marks, *raw, *weights)
    if direct:
        weights, outs = outs[:2], outs[2:]
    weights = [w.reshape(2, D, w.shape[-1]) for w in weights[:2]]
    lse, affine, vec, small = outs[:4]
    arrays = [*outs[4:], weights[0], weights[1], tokens]
    return lse, affine, vec, small, arrays


OUT, FEED, CONTEXT, PAIR, QGRAD, SUMS, ROWS = range(7)
FOLLOW = {
    (OUT, 0): ((0, 0),),
    (FEED, 1): ((1, 0),),
    (FEED, 2): ((0, 1),),
    (FEED, 3): ((2, 0),),
    (FEED, 4): ((1, 1),),
    (FEED, 5): ((0, 2), (2, 1), (3, 0)),
    (FEED, 7): ((4, 0),),
    (PAIR, 0): ((1, 2), (0, 3), (3, 1)),
    (PAIR, 3): ((0, 4), (2, 2), (4, 1), (1, 3)),
    (QGRAD, 0): ((5, 0),),
    (PAIR, 5): ((3, 2), (5, 1)),
    (PAIR, 6): ((1, 4), (2, 3)),
    (QGRAD, 1): ((6, 0),),
    (PAIR, 8): ((4, 2),),
    (PAIR, 9): ((3, 3), (2, 4), (6, 1)),
    (PAIR, 10): ((5, 2),),
    (QGRAD, 2): ((4, 3), (7, 0)),
    (ROWS, 0): ((3, 4), (6, 2)),
    (ROWS, 1): ((5, 3), (7, 1)),
    (ROWS, 3): ((6, 3), (4, 4), (7, 2), (5, 4), (7, 3), (6, 4), (7, 4)),
}


def backward_kernel(direct, *refs):
    affine, marks, lse, small_a = refs[:4]
    hbm_in, refs = dict(zip(LOADED, refs[4 : 4 + len(LOADED)])), refs[4 + len(LOADED) :]
    tokens_grad, refs = refs[0], refs[1:]
    outs, refs = refs[:4], refs[4:]
    small, refs = refs[0], refs[1:]
    held = dict(zip(HELD, refs[: len(HELD)]))
    refs = refs[len(HELD) :]
    ring, resid, grads_out, bias, g_context, g_mix, head_sum = refs[:7]
    load_sem, qkv_sem, ring_sem, resid_sem, out_sem = refs[7:12]
    refs = refs[12:]
    rows_all = bias.shape[0] * SEQ_LEN
    blocks = rows_all // ROW_BLOCK
    loads = {}
    ring_loads = {}

    def load(*names):
        for name in names:
            i = HELD.index(name)
            loads[name] = []
            if name == QKV_W:
                for k in range(9):
                    kind, col = k % 3, k // 3
                    src = hbm_in[name].at[:, :, pl.ds(384 * kind + 128 * col, 128)]
                    dst = held[name].at[:, :, pl.ds(128 * k, 128)]
                    loads[name].append(pltpu.make_async_copy(src, dst, qkv_sem.at[k]))
            else:
                copy = pltpu.make_async_copy(hbm_in[name], held[name], load_sem.at[i])
                loads[name].append(copy)
            for copy in loads[name]:
                copy.start()

    def have(*names):
        for name in names:
            for copy in loads.pop(name, []):
                copy.wait()

    def load_ring(i):
        name, at = (ACTIV, i) if i < 4 else (G_PRE, i - 4)
        start = (at % 2) * 1536 + (at // 2) * 768
        ring_loads[i] = pltpu.make_async_copy(
            hbm_in[name].at[:, pl.ds(start, 768)], ring.at[i % 3], ring_sem.at[i]
        )
        ring_loads[i].start()

    load(G_ATTN, CONTEXTS)
    if direct:
        bufs = [refs[7 * i : 7 * i + 7] for i in range(5)]
        refs = refs[35:]
        scatter = Scatter(SCATTER_CHUNKS, outs, bufs, *refs[:2])
        greet()
    mask_into(bias, marks)
    head_sum[...] = jnp.zeros_like(head_sum)

    def put(chunk, half, value):
        which, start, size = SCATTER_CHUNKS[chunk][:3]
        if direct:
            scatter.fill(chunk, half, value)
        elif which == 0:
            for kind in range(3):
                part = value[:, 128 * kind : 128 * (kind + 1)].astype(BF)
                outs[0][half, :, pl.ds(384 * kind + start, 128)] = part
        else:
            outs[which][half, :, pl.ds(start, size)] = value.astype(BF)

    def comm(piece, i=0):
        if direct:
            for chunk, phase in FOLLOW.get((piece, i), ()):
                scatter.phase(chunk, phase)

    tokens_t, g_attn_t = held[G_FFN_T], held[NORMED_T]
    have(G_ATTN, CONTEXTS)
    load(G_FFN_T)
    load_ring(0)
    load_ring(1)
    for i in range(blocks):
        rows = slice(i * ROW_BLOCK, (i + 1) * ROW_BLOCK)
        g_attn_t[:, rows] = jnp.transpose(held[G_ATTN][rows, :])
    for t in range(2):
        put(0, t, dot(g_attn_t[...], held[CONTEXTS][t]))
    if direct:
        met()
    comm(OUT)
    for i in range(8):
        left = held[G_FFN_T if i < 4 else NORMED_T]
        have(G_FFN_T if i < 4 else NORMED_T)
        ring_loads.pop(i).wait()
        if i == 0:
            load_ring(2)
            load(NORMED_T)
        if i == 2:
            load(OUT_W, MIX)
        if i == 4:
            load(TOKENS)
        if i == 6:
            load(QKV_W)
        put(1 + i // 2, i % 2, dot(left[...], ring[i % 3]))
        if i < 5:
            load_ring(i + 3)
        comm(FEED, i)

    have(OUT_W)

    @pl.loop(0, blocks)
    def _(i):
        rows = pl.ds(pl.multiple_of(i * ROW_BLOCK, ROW_BLOCK), ROW_BLOCK)
        for t in range(2):
            g_context[t, rows, :] = dot(held[G_ATTN][rows, :], held[OUT_W][t]).astype(BF)

    comm(CONTEXT)
    have(MIX, TOKENS)
    for i in range(blocks):
        rows = slice(i * ROW_BLOCK, (i + 1) * ROW_BLOCK)
        tokens_t[:, rows] = jnp.transpose(held[TOKENS][rows, :])
    begin = 0
    for end in range(12):
        if (PAIR, end) not in FOLLOW and end % 4 < 3:
            continue

        @pl.loop(begin, end + 1)
        def _(m):
            attend_back(m, held[MIX], bias, lse, g_context, affine, g_mix, head_sum)

        begin = end + 1
        if end % 4 == 3:
            comm(PAIR, end)
            col = end // 4
            if direct and col < 2:
                scatter.release(col)
            for t in range(2):
                put(5 + col, t, dot(tokens_t[...], g_mix[t, :, 384 * col : 384 * (col + 1)]))
            comm(QGRAD, col)
        else:
            comm(PAIR, end)

    small_in = small if not direct else refs[2].at[0]
    small_in[...] = small_a[...]
    ones = jnp.ones((8, rows_all), BF)
    for t in range(2):
        sums = dot(ones, g_mix[t])
        for col in range(3):
            at = slice(384 * t + 128 * col, 384 * t + 128 * (col + 1))
            small_in[17:18, at] = sums[0:1, 384 * col : 384 * col + 128]
            small_in[18:19, at] = sums[0:1, 384 * col + 256 : 384 * col + 384]
        at = slice(384 * t, 384 * (t + 1))
        small_in[19:20, at] = head_sum[t, 0:1, :] / affine[t, 1:2, 768:1152]
    if direct:
        little = Small(small, *refs[2:7])
        little.step()
    comm(SUMS)
    have(QKV_W)

    def resid_load(i):
        rows = pl.ds(i * ROW_BLOCK, ROW_BLOCK)
        return pltpu.make_async_copy(hbm_in[G_RESID].at[rows], resid.at[i % 2], resid_sem.at[i])

    def out_copy(i):
        rows = pl.ds(i * ROW_BLOCK, ROW_BLOCK)
        return pltpu.make_async_copy(grads_out.at[i % 2], tokens_grad.at[rows], out_sem.at[i])

    resid_load(0).start()
    for i in range(blocks):
        if i + 1 < blocks:
            resid_load(i + 1).start()
        resid_load(i).wait()
        if i >= 2:
            out_copy(i - 2).wait()
        rows = slice(i * ROW_BLOCK, (i + 1) * ROW_BLOCK)
        grads_out[i % 2] = resid[i % 2] + (
            dot(g_mix[0, rows, :], held[QKV_W][0], NT) + dot(g_mix[1, rows, :], held[QKV_W][1], NT)
        )
        out_copy(i).start()
        if direct:
            little.step()
        comm(ROWS, i)
    for i in range(max(0, blocks - 2), blocks):
        out_copy(i).wait()
    if direct:
        little.finish()
        scatter.finish()


HELD = (G_ATTN, CONTEXTS, G_FFN_T, NORMED_T, OUT_W, MIX, TOKENS, QKV_W)
LOADED = HELD + (ACTIV, G_PRE, G_RESID)


def backward_call(direct, affine, marks, lse, small_a, arrays):
    rows = arrays[TOKENS].shape[0]
    seqs = rows // SEQ_LEN
    blocks = rows // ROW_BLOCK
    scratch = [pltpu.VMEM(arrays[name].shape, arrays[name].dtype) for name in HELD]
    scratch += [
        pltpu.VMEM((3, rows, 768), BF),
        pltpu.VMEM((2, ROW_BLOCK, D), F32),
        pltpu.VMEM((2, ROW_BLOCK, D), F32),
        pltpu.VMEM((seqs, SEQ_LEN, SEQ_LEN), F32),
        pltpu.VMEM((2, rows, 384), BF),
        pltpu.VMEM((2, rows, 1152), BF),
        pltpu.VMEM((2, 8, 384), F32),
        pltpu.SemaphoreType.DMA((len(HELD),)),
        pltpu.SemaphoreType.DMA((9,)),
        pltpu.SemaphoreType.DMA((8,)),
        pltpu.SemaphoreType.DMA((blocks,)),
        pltpu.SemaphoreType.DMA((blocks,)),
    ]
    if direct:
        scratch += Scatter.scratch((768,) * 4 + (384,)) + Scatter.semaphores(SCATTER_CHUNKS)
        scratch += Small.scratch()
        extra = dict(collective_id=2, has_side_effects=True)
        grads = [jax.ShapeDtypeStruct((3, 48, 384), F32)]
        grads += [jax.ShapeDtypeStruct((48, w), F32) for w in WIDTHS[1:]]
    else:
        extra = {}
        grads = [jax.ShapeDtypeStruct((2, D, w), BF) for w in WIDTHS]
    tokens_grad, *grads, small = pl.pallas_call(
        functools.partial(backward_kernel, direct),
        out_shape=[
            jax.ShapeDtypeStruct((rows, D), F32),
            *grads,
            jax.ShapeDtypeStruct((SMALL_ROWS, D), F32),
        ],
        in_specs=vmem(4) + hbm(len(LOADED)),
        out_specs=hbm(1) + vmem(5),
        scratch_shapes=scratch,
        compiler_params=pltpu.CompilerParams(vmem_limit_bytes=VMEM_BYTES, **extra),
        name="backward",
    )(affine, marks, lse, small_a, *[arrays[name] for name in LOADED])
    return tokens_grad, grads, small


def finish_kernel(tokens_all, *refs):
    logits, noises = refs[:4], refs[4:8]
    scales, small = refs[8:10]
    grads, refs = refs[10:14], refs[14:]
    outs, refs = refs[:4], refs[4:]
    loss, qkv_b, out_b, up_b, down_b, gain1, shift1, gain2, shift2 = refs[:9]
    head, unit, width, layer = refs[9:]
    for src, dst in zip(grads, outs):
        dst[...] = src[...]
    zh, zu, zw, zl = (gate(flat_row(n), flat_row(v)) for n, v in zip(noises, logits))
    slope = lambda z: z * (1.0 - z) * 1.5

    def row(k):
        return small[k : k + 1, :]

    def put(ref, value):
        ref[...] = value.reshape(ref.shape)

    put(loss, jnp.sum(row(8), axis=1, keepdims=True) * (0.5 / tokens_all))
    qkv_b[...] = small[17:19, :]
    put(out_b, row(0) * scales[1:2, :])
    put(down_b, row(2) * scales[5:6, :])
    for k, ref in ((4, gain1), (5, shift1), (6, gain2), (7, shift2)):
        put(ref, row(k))
    put(up_b, jnp.concatenate([row(9 + j) for j in range(4)], axis=1))
    put(unit, jnp.concatenate([row(13 + j) for j in range(4)], axis=1) * slope(zu))
    put(width, (row(1) * zl[:, 0:1] + row(3) * zl[:, 1:2]) * slope(zw))
    at = lax.broadcasted_iota(jnp.int32, (1, 2), 1)
    first = jnp.sum(row(1) * zw, axis=1, keepdims=True)
    second = jnp.sum(row(3) * zw, axis=1, keepdims=True)
    put(layer, jnp.where(at == 0, first, second) * slope(zl))
    at = lax.broadcasted_iota(jnp.int32, (1, HEADS), 1)
    feature = lax.broadcasted_iota(jnp.int32, (1, D), 1) // HEAD_DIM
    total = jnp.zeros((1, HEADS), F32)
    for h in range(HEADS):
        mine = jnp.sum(jnp.where(feature == h, row(19), 0.0), axis=1, keepdims=True)
        total = jnp.where(at == h, mine, total)
    put(head, total * slope(zh))


def finish_call(tokens_all, raw, vec, small, grads):
    sizes = [1, 0, D, FF, D, D, D, D, D, HEADS, FF, D, 2]
    shapes = [jax.ShapeDtypeStruct(g.shape, F32) for g in grads]
    shapes += [jax.ShapeDtypeStruct((n,) if n else (2, D), F32) for n in sizes]
    return pl.pallas_call(
        functools.partial(finish_kernel, tokens_all),
        out_shape=shapes,
        in_specs=vmem(14),
        out_specs=vmem(17),
        name="finish",
    )(*raw[LOGITS:], vec, small, *grads)


GATHER_CHUNKS = (
    (0, 0, 384),
    (0, 384, 384),
    (0, 768, 384),
    (1, 0, 384),
    (2, 0, 768),
    (2, 768, 768),
    (3, 0, 768),
    (3, 768, 768),
)
SCATTER_CHUNKS = (
    (1, 0, 384, 4, 0),
    (3, 0, 768, 0, 0),
    (3, 768, 768, 1, 0),
    (2, 0, 768, 2, 0),
    (2, 768, 768, 3, 0),
    (0, 0, 384, 4, 0),
    (0, 128, 384, 0, 0),
    (0, 256, 384, 0, 384),
)


def body(direct, tokens, teacher, segments, qkv_weight, qkv_bias, out_weight, out_bias, *args):
    up_weight, up_bias, down_weight, *args = args
    raw = (qkv_bias, out_bias, up_bias, *args)
    kinds = jnp.transpose(qkv_weight, (1, 0, 2))
    weights = [kinds, out_weight, up_weight, down_weight]
    if not direct:
        weights[0] = qkv_weight.reshape(-1, 1152)
        weights = [
            lax.all_gather(lax.all_gather(s, "dp", axis=0, tiled=True), "tensor", axis=0)
            for s in weights
        ]
    lse, affine, vec, small_a, arrays = forward_call(
        direct, tokens, teacher, segments, raw, weights
    )
    tokens_grad, grads, small = backward_call(direct, affine, segments, lse, small_a, arrays)
    if not direct:
        grads = [
            lax.psum_scatter(
                lax.psum_scatter(g, "tensor", scatter_dimension=0),
                "dp",
                scatter_dimension=0,
                tiled=True,
            ).astype(F32)
            for g in grads
        ]
        grads[0] = jnp.transpose(grads[0].reshape(-1, 3, 384), (1, 0, 2))
        small = lax.psum(small, ("dp", "tensor"))
    all_tokens = tokens.shape[0] * lax.axis_size("dp") * lax.axis_size("tensor")
    outs = finish_call(all_tokens, raw, vec, small, grads)
    qkv_grad, out_grad, up_grad, down_grad, loss, qkv_b, out_b, up_b, down_b = outs[:9]
    return (
        arrays[ACTIVATIONS],
        loss.reshape(()),
        tokens_grad,
        jnp.transpose(qkv_grad, (1, 0, 2)),
        qkv_b,
        out_grad,
        out_b,
        up_grad,
        up_b,
        down_grad,
        down_b,
        *outs[9:],
    )


def solution(mesh):
    rows, split, whole = P(("dp", "tensor"), None), P("dp", "tensor"), P()
    cube = P("dp", None, "tensor")
    in_specs = (rows, rows, rows, cube, whole, split, whole, split, whole, split) + (whole,) * 13
    out_specs = (
        rows,
        whole,
        rows,
        cube,
        whole,
        split,
        whole,
        split,
        whole,
        split,
    ) + (whole,) * 9
    direct = mesh.shape["dp"] == 16 and mesh.shape["tensor"] == 2
    return jax.shard_map(
        functools.partial(body, direct),
        mesh=mesh,
        in_specs=in_specs,
        out_specs=out_specs,
        check_vma=False,
    )
```

```python
import functools

import jax
import jax.numpy as jnp
from jax import lax
from jax.experimental import pallas as pl
from jax.experimental.pallas import tpu as pltpu
from jax.sharding import PartitionSpec as P

D = 768
HEADS = 12
HEAD_DIM = 64
FF = 3072
SEQ_LEN = 512
BETA = 2.0 / 3.0
EPS = 1e-12
NEG = -1e30
BF = jnp.bfloat16
F32 = jnp.float32
MESH = pl.DeviceIdType.MESH
VMEM_BYTES = 60 * 1024 * 1024
WIDTHS = (1152, 384, 1536, 1536)
ROW_BLOCK = 256
SMALL_ROWS = 24
NT = (((1,), (1,)), ((), ()))
TN = (((0,), (0,)), ((), ()))
NN = (((1,), (0,)), ((), ()))


def dot(left, right, dims=NN):
    return lax.dot_general(left, right, dims, preferred_element_type=F32)


def vmem(n=1):
    return [pl.BlockSpec(memory_space=pltpu.VMEM)] * n


def hbm(n=1):
    return [pl.BlockSpec(memory_space=pl.ANY)] * n


def coords():
    dp = lax.axis_index("dp")
    return dp // 4, lax.rem(dp // 2, 2), lax.axis_index("tensor"), lax.rem(dp, 2)


def place(z, x, y, c):
    return ((z * 2 + x) * 2 + c, y)


def partners():
    z, x, y, c = coords()
    along = [(lax.rem(z + k, 4), x, y, c) for k in (1, 2, 3)]
    return along + [(z, 1 - x, y, c), (z, x, 1 - y, c), (z, x, y, 1 - c)]


def greet():
    barrier = pltpu.get_barrier_semaphore()
    for partner in partners():
        pl.semaphore_signal(barrier, inc=1, device_id=place(*partner), device_id_type=MESH)


def met():
    pl.semaphore_wait(pltpu.get_barrier_semaphore(), 6)


class Gather:
    COPIES = 12

    def __init__(self, chunks, ins, outs, local_sem, send_sem, recv_sem):
        self.chunks, self.ins, self.outs = chunks, ins, outs
        self.local_sem, self.send_sem, self.recv_sem = local_sem, send_sem, recv_sem
        self.kept = {}
        self.started = []
        self.locals = {}

    def send(self, chunk, slot, src, dst, target):
        copy = pltpu.make_async_remote_copy(
            src_ref=src,
            dst_ref=dst,
            send_sem=self.send_sem.at[chunk, slot],
            recv_sem=self.recv_sem.at[chunk, slot],
            device_id=place(*target),
            device_id_type=MESH,
        )
        copy.start()
        self.started.append(copy)
        self.kept[chunk, slot] = copy

    def arrived(self, chunk, *slots):
        for slot in slots:
            self.kept[chunk, slot].wait_recv()

    def source(self, chunk):
        which, start, size, _ = self.chunks[chunk]
        if which == 0:
            return self.ins[0].at[start // size]
        return self.ins[which].at[:, pl.ds(start, size)]

    def target(self, chunk):
        which, start, size, _ = self.chunks[chunk]
        z, x, y, c = coords()
        return self.outs[which].at[y, z, x, c, :, pl.ds(start, size)]

    def own(self):
        for i in range(len(self.chunks)):
            copy = pltpu.make_async_copy(self.source(i), self.target(i), self.local_sem.at[i])
            copy.start()
            self.locals[i] = copy

    def phase(self, chunk, phase):
        z, x, y, c = coords()
        across, beside, core = (z, 1 - x, y, c), (z, x, 1 - y, c), (z, x, y, 1 - c)
        which, start, size, flat_first = self.chunks[chunk]
        cols = pl.ds(start, size)
        out = self.outs[which]

        def pass_on(slot, view, target):
            self.send(chunk, slot, view, view, target)

        if flat_first:
            if phase == 0:
                self.send(chunk, 0, self.source(chunk), self.target(chunk), across)
                self.send(chunk, 1, self.source(chunk), self.target(chunk), beside)
            elif phase == 1:
                self.arrived(chunk, 0, 1)
                t, v = y + c * (1 - 2 * y), 1 - x + c * (2 * x - 1)
                pass_on(2, out.at[t, z, v, c, :, cols], (z, 1 - v, 1 - t, c))
            elif phase == 2:
                self.locals[chunk].wait()
                self.arrived(chunk, 2)
                for k in range(3):
                    to = lax.rem(z + k + 1, 4)
                    pass_on(3 + k, out.at[:, z, :, c, :, cols], (to, x, y, c))
            elif phase == 3:
                self.arrived(chunk, 3, 4, 5)
                pass_on(6, out.at[:, :, :, c, :, cols], core)
            else:
                self.arrived(chunk, 6)
            return
        if phase == 0:
            for k in range(3):
                self.send(
                    chunk,
                    k,
                    self.source(chunk),
                    self.target(chunk),
                    (lax.rem(z + k + 1, 4), x, y, c),
                )
        elif phase == 1:
            self.locals[chunk].wait()
            self.arrived(chunk, 0, 1, 2)
            pass_on(3, out.at[y, 0:2, x, c, :, cols], across)
            pass_on(4, out.at[y, 2:4, x, c, :, cols], beside)
            pass_on(7, out.at[y, :, x, c, :, cols], core)
        elif phase == 2:
            self.arrived(chunk, 3)
            pass_on(5, out.at[y, 0:2, :, c, :, cols], beside)
            self.arrived(chunk, 4)
            pass_on(6, out.at[:, 2:4, x, c, :, cols], across)
            pass_on(8, out.at[y, 0:2, 1 - x, c, :, cols], core)
            pass_on(9, out.at[1 - y, 2:4, x, c, :, cols], core)
        elif phase == 3:
            self.arrived(chunk, 5)
            pass_on(10, out.at[1 - y, 0:2, :, c, :, cols], core)
            self.arrived(chunk, 6)
            pass_on(11, out.at[:, 2:4, 1 - x, c, :, cols], core)
        else:
            self.arrived(chunk, 7, 8, 9, 10, 11)

    def finish(self):
        for copy in self.started:
            copy.wait_send()


class Scatter:
    COPIES = 8

    def __init__(self, chunks, outs, bufs, send_sem, recv_sem):
        self.chunks, self.outs, self.bufs = chunks, outs, bufs
        self.send_sem, self.recv_sem = send_sem, recv_sem
        self.kept = {}
        self.started = {}

    def send(self, chunk, slot, src, dst, target):
        copy = pltpu.make_async_remote_copy(
            src_ref=src,
            dst_ref=dst,
            send_sem=self.send_sem.at[chunk, slot],
            recv_sem=self.recv_sem.at[chunk, slot],
            device_id=place(*target),
            device_id_type=MESH,
        )
        copy.start()
        self.started.setdefault(chunk, []).append(copy)
        self.kept[chunk, slot] = copy

    def arrived(self, chunk, *slots):
        for slot in slots:
            self.kept[chunk, slot].wait_recv()

    def release(self, chunk):
        for copy in self.started.pop(chunk, []):
            copy.wait_send()

    def views(self, chunk):
        _, _, size, at, lane = self.chunks[chunk]
        return tuple(
            ref.at[(slice(None),) * (len(ref.shape) - 1) + (pl.ds(lane, size),)]
            for ref in self.bufs[at]
        )

    def fill(self, chunk, half, value):
        c = coords()[3]
        both = self.views(chunk)[0]
        for i in range(16):
            z, x, k = i // 4, (i // 2) % 2, i % 2
            side = lax.rem(c + k, 2)
            both[side, half, z, x] = value[48 * i : 48 * (i + 1), :].astype(BF)

    def phase(self, chunk, phase):
        z, x, y, c = coords()
        across, beside, core = (z, 1 - x, y, c), (z, x, 1 - y, c), (z, x, y, 1 - c)
        both, first, low_a, low_b, last_a, last_b, last = self.views(chunk)
        sums = both.at[0]

        def add(left, right):
            left[...] = (left[...].astype(F32) + right[...].astype(F32)).astype(BF)

        if phase == 0:
            self.send(chunk, 0, both.at[1], first, core)
        elif phase == 1:
            self.arrived(chunk, 0)

            @pl.loop(0, 16)
            def _(i):
                at = (i // 8, lax.rem(i // 2, 4), lax.rem(i, 2))
                add(sums.at[at], first.at[at])

            self.send(chunk, 1, sums.at[1 - y, 0:2], low_a, beside)
            self.send(chunk, 2, sums.at[:, 2:4, 1 - x], low_b, across)
        elif phase == 2:
            self.arrived(chunk, 1)

            @pl.loop(0, 4)
            def _(i):
                k, v = i // 2, lax.rem(i, 2)
                add(sums.at[y, k, v], low_a.at[k, v])

            self.send(chunk, 3, sums.at[y, 0:2, 1 - x], last_a, across)
            self.arrived(chunk, 2)

            @pl.loop(0, 4)
            def _(i):
                t, k = i // 2, lax.rem(i, 2)
                add(sums.at[t, k + 2, x], low_b.at[t, k])

            self.send(chunk, 4, sums.at[1 - y, 2:4, x], last_b, beside)
        elif phase == 3:
            self.arrived(chunk, 3, 4)

            @pl.loop(0, 2)
            def _(k):
                add(sums.at[y, k, x], last_a.at[k])
                add(sums.at[y, k + 2, x], last_b.at[k])

            for k in range(3):
                to = lax.rem(z + k + 1, 4)
                self.send(chunk, 5 + k, sums.at[y, to, x], last.at[k], (to, x, y, c))
        else:
            self.arrived(chunk, 5, 6, 7)
            total = sums[y, z, x].astype(F32)
            for k in range(3):
                total = total + last[k].astype(F32)
            which, start, size = self.chunks[chunk][:3]
            if which == 0:
                for kind in range(3):
                    part = total[:, 128 * kind : 128 * (kind + 1)]
                    self.outs[0][kind, :, pl.ds(start, 128)] = part
            else:
                self.outs[which][:, pl.ds(start, size)] = total

    def finish(self):
        for chunk in list(self.started):
            self.release(chunk)

    @staticmethod
    def scratch(sizes):
        shapes = []
        for n in sizes:
            shapes += [
                pltpu.VMEM((2, 2, 4, 2, 48, n), BF),
                pltpu.VMEM((2, 4, 2, 48, n), BF),
                pltpu.VMEM((2, 2, 48, n), BF),
                pltpu.VMEM((2, 2, 48, n), BF),
                pltpu.VMEM((2, 48, n), BF),
                pltpu.VMEM((2, 48, n), BF),
                pltpu.VMEM((3, 48, n), BF),
            ]
        return shapes

    @staticmethod
    def semaphores(chunks):
        n = len(chunks)
        return [
            pltpu.SemaphoreType.DMA((n, Scatter.COPIES)),
            pltpu.SemaphoreType.DMA((n, Scatter.COPIES)),
        ]


class Small:
    def __init__(self, out, own, got, lines, send_sem, recv_sem):
        self.out, self.own, self.got, self.lines = out, own, got, lines
        self.send_sem, self.recv_sem = send_sem, recv_sem
        self.pending = []
        self.step_at = 0

    def send(self, slot, src, dst, target):
        copy = pltpu.make_async_remote_copy(
            src_ref=src,
            dst_ref=dst,
            send_sem=self.send_sem.at[slot],
            recv_sem=self.recv_sem.at[slot],
            device_id=place(*target),
            device_id_type=MESH,
        )
        copy.start()
        self.pending.append(copy)

    def step(self):
        z, x, y, c = coords()
        nearby = ((z, x, y, 1 - c), (z, 1 - x, y, c), (z, x, 1 - y, c))
        at = self.step_at
        if at > 4:
            return
        self.step_at += 1
        for copy in self.pending:
            copy.wait()
        self.pending = []
        if 1 <= at <= 3:
            self.own[at] = self.own[at - 1] + self.got[at - 1]
        if at < 3:
            self.send(at, self.own.at[at], self.got.at[at], nearby[at])
        elif at == 3:
            self.lines[z] = self.own[3]
            for k in range(3):
                to = (lax.rem(z + k + 1, 4), x, y, c)
                self.send(3 + k, self.own.at[3], self.lines.at[z], to)
        else:
            self.out[...] = (self.lines[0] + self.lines[1]) + (self.lines[2] + self.lines[3])

    def finish(self):
        while self.step_at <= 4:
            self.step()

    @staticmethod
    def scratch():
        return [
            pltpu.VMEM((4, SMALL_ROWS, D), F32),
            pltpu.VMEM((3, SMALL_ROWS, D), F32),
            pltpu.VMEM((4, SMALL_ROWS, D), F32),
            pltpu.SemaphoreType.DMA((6,)),
            pltpu.SemaphoreType.DMA((6,)),
        ]


def head_masks():
    lane = lax.broadcasted_iota(jnp.int32, (SEQ_LEN, 128), 1)
    return lane < HEAD_DIM


def pair_at(i):
    seq, pair = i // 6, lax.rem(i, 6)
    half, col = pair // 3, lax.rem(pair, 3)
    return seq, half, col, pl.ds(pl.multiple_of(seq * SEQ_LEN, SEQ_LEN), SEQ_LEN)


def lanes(col, base):
    return pl.ds(pl.multiple_of(base + col * 128, 128), 128)


def mask_into(bias, marks):
    for s in range(bias.shape[0]):
        item = lax.broadcasted_iota(jnp.int32, (16, SEQ_LEN), 0)
        hot = jnp.where(marks[s : s + 1, :] == item, 1.0, 0.0).astype(BF)
        bias[s] = (dot(hot, hot, TN) - 1.0) * -NEG


def gate(noise, logit):
    return jax.nn.sigmoid((jnp.log(noise) - jnp.log1p(-noise) + logit) * (1.0 / BETA))


def flat_row(ref):
    return ref[...].reshape(1, ref.shape[0])


def over_heads(values):
    head = lax.broadcasted_iota(jnp.int32, (1, D), 1) // HEAD_DIM
    out = jnp.zeros((1, D), F32)
    for h in range(HEADS):
        out = jnp.where(head == h, values[:, h : h + 1], out)
    return out


def prepare(raw, affine, vec, uvec):
    zh = over_heads(gate_of(raw, HEAD))
    zw = gate_of(raw, WIDTH)
    zl = gate_of(raw, LAYER)
    for t in range(2):
        cols = slice(384 * t, 384 * (t + 1))
        affine[t, 0:1, 0:384] = raw[QKV_BIAS][0:1, cols]
        affine[t, 0:1, 384:768] = jnp.zeros((1, 384), F32)
        affine[t, 0:1, 768:1152] = raw[QKV_BIAS][1:2, cols]
        affine[t, 1:2, 0:384] = jnp.full((1, 384), HEAD_DIM**-0.5, F32)
        affine[t, 1:2, 384:768] = jnp.ones((1, 384), F32)
        affine[t, 1:2, 768:1152] = zh[:, cols]
    for i, name in enumerate(VEC):
        vec[i : i + 1, :] = zl[:, i // 4 : i // 4 + 1] * zw if name is None else flat_row(raw[name])
    uvec[0:1, :] = flat_row(raw[UP_BIAS])
    uvec[1:2, :] = gate_of(raw, UNIT)


QKV_BIAS, OUT_BIAS, UP_BIAS, DOWN_BIAS, GAIN1, SHIFT1, GAIN2, SHIFT2 = range(8)
LOGITS, NOISES = 8, 12
HEAD, UNIT, WIDTH, LAYER = range(4)
PREP = 16
VEC = (OUT_BIAS, None, GAIN1, SHIFT1, DOWN_BIAS, None, GAIN2, SHIFT2)


def gate_of(raw, kind):
    return gate(flat_row(raw[NOISES + kind]), flat_row(raw[LOGITS + kind]))


def project(i, tokens, weight, affine, mix):
    rows = pl.ds(pl.multiple_of(i * ROW_BLOCK, ROW_BLOCK), ROW_BLOCK)
    for t in range(2):
        mixed = dot(tokens[rows, :], weight(t))
        mix[t, rows, :] = ((mixed + affine[t, 0:1, :]) * affine[t, 1:2, :]).astype(BF)


def attend(i, mix, bias, context, lse):
    left = head_masks()
    seq, t, col, rows = pair_at(i)
    query = mix[t, rows, lanes(col, 0)]
    keys = mix[t, rows, lanes(col, 384)]
    values = mix[t, rows, lanes(col, 768)]
    parts = []
    for h in range(2):
        mine = jnp.where(left if h == 0 else ~left, query, 0)
        scores = dot(mine, keys, NT) + bias[seq]
        top = jnp.max(scores, axis=1, keepdims=True)
        expo = jnp.exp(scores - top)
        total = jnp.sum(expo, axis=1, keepdims=True)
        probs = (expo * (1.0 / total)).astype(BF)
        parts.append(dot(probs, values))
        logsum = jnp.broadcast_to(top + jnp.log(total), (SEQ_LEN, 128))
        lse[i, h : h + 1, :] = jnp.transpose(logsum)[0:1, :]
    context[t, rows, lanes(col, 0)] = jnp.where(left, parts[0], parts[1]).astype(BF)


def attend_back(m, mix, bias, lse, g_context, affine, g_mix, head_sum):
    left = head_masks()
    seq, t, col = lax.rem(m, 2), lax.rem(m // 2, 2), m // 4
    i = seq * 6 + t * 3 + col
    rows = pl.ds(pl.multiple_of(seq * SEQ_LEN, SEQ_LEN), SEQ_LEN)
    query = mix[t, rows, lanes(col, 0)]
    keys = mix[t, rows, lanes(col, 384)]
    values = mix[t, rows, lanes(col, 768)]
    grad = g_context[t, rows, lanes(col, 0)]
    parts = []
    for h in range(2):
        side = left if h == 0 else ~left
        scores = dot(jnp.where(side, keys, 0), query, NT) + bias[seq]
        probs = jnp.exp(scores - lse[i, h : h + 1, :])
        g_probs = dot(jnp.where(side, values, 0), grad, NT)
        delta = jnp.sum(g_probs * probs, axis=0, keepdims=True)
        g_scores = (probs * (g_probs - delta)).astype(BF)
        parts.append(
            (
                dot(g_scores, keys, TN),
                dot(g_scores, query),
                dot(probs.astype(BF), grad),
            )
        )
    g_query, g_keys, g_values = (jnp.where(left, a, b) for a, b in zip(*parts))
    g_mix[t, rows, lanes(3 * col, 0)] = (g_query * HEAD_DIM**-0.5).astype(BF)
    g_mix[t, rows, lanes(3 * col, 128)] = g_keys.astype(BF)
    used = affine[t, 1:2, lanes(col, 768)]
    g_mix[t, rows, lanes(3 * col, 256)] = (g_values * used).astype(BF)
    used = jnp.sum(g_values * values.astype(F32), axis=0, keepdims=True)
    head_sum[t, 0:1, lanes(col, 0)] += used


def normalise(value):
    mean = jnp.mean(value, axis=1, keepdims=True)
    centred = value - mean
    var = jnp.mean(centred * centred, axis=1, keepdims=True)
    rstd = lax.rsqrt(var + EPS)
    return centred * rstd, rstd


def norm_back(grad, unit, rstd):
    mean = jnp.mean(grad, axis=1, keepdims=True)
    along = jnp.mean(grad * unit, axis=1, keepdims=True)
    return rstd * (grad - mean - unit * along)


def fold(value):
    return jnp.sum(value.reshape(value.shape[0] // 8, 8, value.shape[1]), axis=0)


START, PROJECT, PAIRS, UP = range(4)
ARRIVE = {
    (START, 0): ((0, 0), (1, 0), (7, 0), (7, 1), (0, 1), (1, 1), (2, 0), (3, 0), (0, 2), (1, 2), (2, 1), (4, 0), (3, 1), (5, 0), (0, 3), (1, 3), (2, 2), (0, 4), (1, 4), (3, 2), (4, 1), (6, 0), (2, 3), (2, 4)),
    (PROJECT, 0): ((5, 1), (7, 2)),
    (PAIRS, 1): ((4, 2),),
    (PAIRS, 4): ((3, 3), (6, 1)),
    (PAIRS, 6): ((5, 2),),
    (PAIRS, 9): ((3, 4),),
    (PAIRS, 11): ((7, 3), (6, 2), (7, 4), (4, 3), (4, 4)),
    (UP, 0): ((5, 3),),
    (UP, 1): ((5, 4), (6, 3)),
    (UP, 2): ((6, 4),),
}


def spans(direct, kind, count):
    begin = 0
    for i in range(count):
        if (direct and (kind, i) in ARRIVE) or i == count - 1:
            yield begin, i + 1
            begin = i + 1


def forward_kernel(direct, *refs):
    tokens, teacher, marks = refs[:3]
    raw = refs[3 : 3 + PREP]
    refs = refs[3 + PREP :]
    weights, refs = refs[:4], refs[4:]
    if direct:
        full, refs = refs[:2], refs[2:]
    lse, affine, vec, small = refs[:4]
    out = refs[4 : 4 + STREAMED]
    refs = refs[4 + STREAMED :]
    held, refs = refs[:4], refs[4:]
    mix, context, attn, bias, uvec, deriv, activ = refs[:7]
    normed_t, g_ffn_t, result_low, g_attn, sums, unit_sums = refs[7:13]
    keep_sem, load_sem, stream_sem = refs[13:16]
    refs = refs[16:]
    rows_all = tokens.shape[0]
    blocks = rows_all // ROW_BLOCK
    if direct:
        gather = Gather(GATHER_CHUNKS, weights, held, *refs)
        greet()
        gather.own()
        prepare(raw, affine, vec, uvec)
        met()
    else:
        loads = [pltpu.make_async_copy(*pair, load_sem.at[i]) for i, pair in enumerate(zip(weights, held))]
        for copy in loads:
            copy.start()
        prepare(raw, affine, vec, uvec)
        for copy in loads:
            copy.wait()
    mask_into(bias, marks)
    sums[...] = jnp.zeros_like(sums)
    unit_sums[...] = jnp.zeros_like(unit_sums)

    def weight(which, t):
        return held[which][t].reshape(D, WIDTHS[which])

    def comm(piece, i=0):
        if direct:
            for chunk, phase in ARRIVE.get((piece, i), ()):
                gather.phase(chunk, phase)

    kept = []

    def keep(src, dst):
        copy = pltpu.make_async_copy(src, dst, keep_sem.at[len(kept)])
        copy.start()
        kept.append(copy)

    def row_span(i):
        start = i * ROW_BLOCK
        return pl.ds(start if isinstance(i, int) else pl.multiple_of(start, ROW_BLOCK), ROW_BLOCK)

    def stream(name, i):
        rows = row_span(i)
        across = out[name].at[:, rows] if name in (NORMED_T, G_FFN_T) else out[name].at[rows]
        source = {
            ACTIVATIONS: result_low,
            G_ATTN: g_attn,
            G_RESID: attn,
            ACTIV: activ,
            G_PRE: activ,
        }
        if name in source:
            src = source[name].at[rows]
        else:
            src = (normed_t if name == NORMED_T else g_ffn_t).at[i]
        return pltpu.make_async_copy(src, across, stream_sem.at[name, i])

    comm(START)
    if direct:
        keep(held[0], full[0])
    for begin, end in spans(direct, PROJECT, blocks):

        @pl.loop(begin, end)
        def _(i):
            project(i, tokens, lambda t: weight(0, t), affine, mix)

        comm(PROJECT, end - 1)
    for begin, end in spans(direct, PAIRS, 12):

        @pl.loop(begin, end)
        def _(i):
            attend(i, mix, bias, context, lse)

        comm(PAIRS, end - 1)
    if direct:
        keep(held[1], full[1])
    keep(mix, out[MIX])
    keep(context, out[CONTEXTS])
    out_bias, scale1, gain1, shift1 = (vec[i : i + 1, :] for i in range(4))
    down_bias, scale2, gain2, shift2 = (vec[i : i + 1, :] for i in range(4, 8))

    def upward(i):
        rows = row_span(i)
        both = dot(context[0, rows, :], weight(1, 0), NT) + dot(context[1, rows, :], weight(1, 1), NT)
        attn[rows, :] = both
        unit1, _ = normalise(tokens[rows, :].astype(F32) + (both + out_bias) * scale1)
        normed_low = (unit1 * gain1 + shift1).astype(BF)
        normed_t[i] = jnp.transpose(normed_low)
        stream(NORMED_T, i).start()
        for t in range(2):
            flat = slice(1536 * t, 1536 * (t + 1))
            pre = dot(normed_low, weight(2, t)) + uvec[0:1, flat]
            gates = uvec[1:2, flat]
            phi = 0.5 + 0.5 * lax.erf(pre * (0.5**0.5))
            pdf = jnp.exp(pre * pre * -0.5) * ((2.0 * jnp.pi) ** -0.5)
            deriv[rows, flat] = (phi + pre * pdf) * gates
            activ[rows, flat] = (pre * phi * gates).astype(BF)
        stream(ACTIV, i).start()

    if direct:
        for i in range(blocks):
            upward(i)
            comm(UP, i)
    else:
        pl.loop(0, blocks)(upward)

    @pl.loop(0, blocks)
    def _(i):
        rows = row_span(i)
        attn_b = attn[rows, :] + out_bias
        unit1, rstd1 = normalise(tokens[rows, :].astype(F32) + attn_b * scale1)
        normed = unit1 * gain1 + shift1
        ffn_b = (
            dot(activ[rows, 0:1536], weight(3, 0), NT) + dot(activ[rows, 1536:3072], weight(3, 1), NT)
        ) + down_bias
        unit2, rstd2 = normalise(normed + ffn_b * scale2)
        result = unit2 * gain2 + shift2
        result_low[rows, :] = result.astype(BF)
        stream(ACTIVATIONS, i).start()
        diff = result - teacher[rows, :].astype(F32)
        g_value2 = norm_back(diff * gain2, unit2, rstd2)
        g_ffn_low = (g_value2 * scale2).astype(BF)
        g_ffn_t[i] = jnp.transpose(g_ffn_low)
        stream(G_FFN_T, i).start()
        sums[2] += fold(g_value2)
        sums[3] += fold(g_value2 * ffn_b)
        sums[6] += fold(diff * unit2)
        sums[7] += fold(diff)
        sums[8] += fold(diff * diff)
        ones = jnp.ones((8, ROW_BLOCK), BF)
        stream(ACTIV, i).wait()
        g_normed = g_value2
        for t in range(2):
            flat = slice(1536 * t, 1536 * (t + 1))
            g_activ = dot(g_ffn_low, weight(3, t))
            unit_sums[0, :, flat] += fold(g_activ * activ[rows, flat].astype(F32))
            grad = (g_activ * deriv[rows, flat]).astype(BF)
            activ[rows, flat] = grad
            unit_sums[1, :, flat] += dot(ones, grad)
            g_normed = g_normed + dot(grad, weight(2, t), NT)
        stream(G_PRE, i).start()
        g_value1 = norm_back(g_normed * gain1, unit1, rstd1)
        attn[rows, :] = g_value1
        stream(G_RESID, i).start()
        g_attn[rows, :] = (g_value1 * scale1).astype(BF)
        stream(G_ATTN, i).start()
        sums[0] += fold(g_value1)
        sums[1] += fold(g_value1 * attn_b)
        sums[4] += fold(g_normed * unit1)
        sums[5] += fold(g_normed)

    small[...] = jnp.zeros_like(small)
    for k in range(9):
        small[k : k + 1, :] = jnp.sum(sums[k], axis=0, keepdims=True)
    for j in range(4):
        cols = slice(768 * j, 768 * (j + 1))
        small[9 + j : 10 + j, :] = unit_sums[1, 0:1, cols]
        total = jnp.sum(unit_sums[0, :, cols], axis=0, keepdims=True)
        small[13 + j : 14 + j, :] = total / uvec[1:2, cols]
    for name in range(2, STREAMED):
        for i in range(blocks):
            if name != ACTIV:
                stream(name, i).wait()
    for copy in kept:
        copy.wait()
    if direct:
        gather.finish()


MIX, CONTEXTS, ACTIVATIONS, G_ATTN, G_RESID, ACTIV, G_PRE, NORMED_T, G_FFN_T = range(9)
STREAMED = 9
QKV_W, OUT_W, TOKENS = range(9, 12)


def forward_call(direct, tokens, teacher, marks, raw, weights):
    rows = tokens.shape[0]
    seqs = rows // SEQ_LEN
    blocks = rows // ROW_BLOCK
    n = len(GATHER_CHUNKS)
    full = [jax.ShapeDtypeStruct((2, 4, 2, 2, 48, w), BF) for w in WIDTHS]
    shapes = [
        jax.ShapeDtypeStruct((6 * seqs, 8, SEQ_LEN), F32),
        jax.ShapeDtypeStruct((2, 8, 1152), F32),
        jax.ShapeDtypeStruct((8, D), F32),
        jax.ShapeDtypeStruct((SMALL_ROWS, D), F32),
    ]
    streamed = [
        jax.ShapeDtypeStruct((2, rows, 1152), BF),
        jax.ShapeDtypeStruct((2, rows, 384), BF),
        jax.ShapeDtypeStruct((rows, D), BF),
        jax.ShapeDtypeStruct((rows, D), BF),
        jax.ShapeDtypeStruct((rows, D), F32),
        jax.ShapeDtypeStruct((rows, FF), BF),
        jax.ShapeDtypeStruct((rows, FF), BF),
        jax.ShapeDtypeStruct((D, rows), BF),
        jax.ShapeDtypeStruct((D, rows), BF),
    ]
    scratch = [pltpu.VMEM(f.shape, BF) for f in full]
    scratch += [
        pltpu.VMEM((2, rows, 1152), BF),
        pltpu.VMEM((2, rows, 384), BF),
        pltpu.VMEM((rows, D), F32),
        pltpu.VMEM((seqs, SEQ_LEN, SEQ_LEN), F32),
        pltpu.VMEM((8, FF), F32),
        pltpu.VMEM((rows, FF), F32),
        pltpu.VMEM((rows, FF), BF),
        pltpu.VMEM((blocks, D, ROW_BLOCK), BF),
        pltpu.VMEM((blocks, D, ROW_BLOCK), BF),
        pltpu.VMEM((rows, D), BF),
        pltpu.VMEM((rows, D), BF),
        pltpu.VMEM((9, 8, D), F32),
        pltpu.VMEM((2, 8, FF), F32),
        pltpu.SemaphoreType.DMA((4,)),
        pltpu.SemaphoreType.DMA((4,)),
        pltpu.SemaphoreType.DMA((STREAMED, blocks)),
    ]
    extra = {}
    if direct:
        scratch += [
            pltpu.SemaphoreType.DMA((n,)),
            pltpu.SemaphoreType.DMA((n, Gather.COPIES)),
            pltpu.SemaphoreType.DMA((n, Gather.COPIES)),
        ]
        extra = dict(collective_id=1, has_side_effects=True)
    else:
        weights = [w.reshape(f.shape) for w, f in zip(weights, full)]
    outs = pl.pallas_call(
        functools.partial(forward_kernel, direct),
        out_shape=(full[:2] if direct else []) + shapes + streamed,
        in_specs=vmem(3 + PREP) + (vmem(4) if direct else hbm(4)),
        out_specs=(hbm(2) if direct else []) + vmem(len(shapes)) + hbm(len(streamed)),
        scratch_shapes=scratch,
        compiler_params=pltpu.CompilerParams(vmem_limit_bytes=VMEM_BYTES, **extra),
        name="forward",
    )(tokens, teacher, marks, *raw, *weights)
    if direct:
        weights, outs = outs[:2], outs[2:]
    weights = [w.reshape(2, D, w.shape[-1]) for w in weights[:2]]
    lse, affine, vec, small = outs[:4]
    arrays = [*outs[4:], weights[0], weights[1], tokens]
    return lse, affine, vec, small, arrays


OUT, FEED, CONTEXT, PAIR, QGRAD, SUMS, ROWS = range(7)
LITTLE = None
FOLLOW = {
    (OUT, 0): ((0, 0),),
    (FEED, 1): ((1, 0),),
    (FEED, 2): ((0, 1),),
    (FEED, 3): ((2, 0),),
    (FEED, 4): ((1, 1),),
    (FEED, 5): ((0, 2), (2, 1), (3, 0)),
    (FEED, 7): ((4, 0),),
    (PAIR, 0): ((1, 2), (0, 3), (3, 1)),
    (PAIR, 3): ((0, 4), (2, 2), (4, 1), (1, 3)),
    (QGRAD, 0): ((5, 0),),
    (PAIR, 5): ((3, 2), (5, 1)),
    (PAIR, 6): ((1, 4), (2, 3)),
    (QGRAD, 1): ((6, 0),),
    (PAIR, 8): ((4, 2),),
    (PAIR, 9): ((3, 3), (2, 4), (6, 1)),
    (PAIR, 10): ((5, 2),),
    (QGRAD, 2): ((4, 3), (7, 0)),
    (ROWS, 0): ((3, 4), (6, 2)),
    (ROWS, 1): ((5, 3), LITTLE, (7, 1)),
    (ROWS, 3): (
        ((6, 3), LITTLE, (4, 4), (7, 2), LITTLE, (5, 4), (7, 3), (6, 4), LITTLE, (7, 4))
    ),
}


def backward_kernel(direct, *refs):
    affine, marks, lse, small_a = refs[:4]
    hbm_in, refs = dict(zip(LOADED, refs[4 : 4 + len(LOADED)])), refs[4 + len(LOADED) :]
    tokens_grad, refs = refs[0], refs[1:]
    outs, refs = refs[:4], refs[4:]
    small, refs = refs[0], refs[1:]
    held = dict(zip(HELD, refs[: len(HELD)]))
    refs = refs[len(HELD) :]
    ring, resid, grads_out, bias, g_context, g_mix, head_sum = refs[:7]
    load_sem, qkv_sem, ring_sem, resid_sem, out_sem = refs[7:12]
    refs = refs[12:]
    rows_all = bias.shape[0] * SEQ_LEN
    blocks = rows_all // ROW_BLOCK
    loads = {}
    ring_loads = {}

    def load(*names):
        for name in names:
            i = HELD.index(name)
            loads[name] = []
            if name == QKV_W:
                for k in range(9):
                    kind, col = k % 3, k // 3
                    src = hbm_in[name].at[:, :, pl.ds(384 * kind + 128 * col, 128)]
                    dst = held[name].at[:, :, pl.ds(128 * k, 128)]
                    loads[name].append(pltpu.make_async_copy(src, dst, qkv_sem.at[k]))
            else:
                copy = pltpu.make_async_copy(hbm_in[name], held[name], load_sem.at[i])
                loads[name].append(copy)
            for copy in loads[name]:
                copy.start()

    def have(*names):
        for name in names:
            for copy in loads.pop(name, []):
                copy.wait()

    def load_ring(i):
        name, at = (ACTIV, i) if i < 4 else (G_PRE, i - 4)
        start = (at % 2) * 1536 + (at // 2) * 768
        ring_loads[i] = pltpu.make_async_copy(
            hbm_in[name].at[:, pl.ds(start, 768)], ring.at[i % 3], ring_sem.at[i]
        )
        ring_loads[i].start()

    load(G_ATTN, CONTEXTS)
    if direct:
        bufs = [refs[7 * i : 7 * i + 7] for i in range(5)]
        refs = refs[35:]
        scatter = Scatter(SCATTER_CHUNKS, outs, bufs, *refs[:2])
        greet()
    mask_into(bias, marks)
    head_sum[...] = jnp.zeros_like(head_sum)

    def put(chunk, half, value):
        which, start, size = SCATTER_CHUNKS[chunk][:3]
        if direct:
            scatter.fill(chunk, half, value)
        elif which == 0:
            for kind in range(3):
                part = value[:, 128 * kind : 128 * (kind + 1)].astype(BF)
                outs[0][half, :, pl.ds(384 * kind + start, 128)] = part
        else:
            outs[which][half, :, pl.ds(start, size)] = value.astype(BF)

    def comm(piece, i=0):
        if direct:
            for at in FOLLOW.get((piece, i), ()):
                if at is LITTLE:
                    little.step()
                else:
                    scatter.phase(*at)

    tokens_t, g_attn_t = held[G_FFN_T], held[NORMED_T]
    have(G_ATTN, CONTEXTS)
    load(G_FFN_T)
    load_ring(0)
    load_ring(1)
    for i in range(blocks):
        rows = slice(i * ROW_BLOCK, (i + 1) * ROW_BLOCK)
        g_attn_t[:, rows] = jnp.transpose(held[G_ATTN][rows, :])
    for t in range(2):
        put(0, t, dot(g_attn_t[...], held[CONTEXTS][t]))
    if direct:
        met()
    comm(OUT)
    for i in range(8):
        left = held[G_FFN_T if i < 4 else NORMED_T]
        have(G_FFN_T if i < 4 else NORMED_T)
        ring_loads.pop(i).wait()
        if i == 0:
            load_ring(2)
            load(NORMED_T)
        if i == 2:
            load(OUT_W, MIX)
        if i == 4:
            load(TOKENS)
        if i == 6:
            load(QKV_W)
        put(1 + i // 2, i % 2, dot(left[...], ring[i % 3]))
        if i < 5:
            load_ring(i + 3)
        comm(FEED, i)

    have(OUT_W)

    @pl.loop(0, blocks)
    def _(i):
        rows = pl.ds(pl.multiple_of(i * ROW_BLOCK, ROW_BLOCK), ROW_BLOCK)
        for t in range(2):
            g_context[t, rows, :] = dot(held[G_ATTN][rows, :], held[OUT_W][t]).astype(BF)

    comm(CONTEXT)
    have(MIX, TOKENS)
    for i in range(blocks):
        rows = slice(i * ROW_BLOCK, (i + 1) * ROW_BLOCK)
        tokens_t[:, rows] = jnp.transpose(held[TOKENS][rows, :])
    begin = 0
    for end in range(12):
        if (PAIR, end) not in FOLLOW and end % 4 < 3:
            continue

        @pl.loop(begin, end + 1)
        def _(m):
            attend_back(m, held[MIX], bias, lse, g_context, affine, g_mix, head_sum)

        begin = end + 1
        if end % 4 == 3:
            comm(PAIR, end)
            col = end // 4
            if direct and col < 2:
                scatter.release(col)
            for t in range(2):
                put(5 + col, t, dot(tokens_t[...], g_mix[t, :, 384 * col : 384 * (col + 1)]))
            comm(QGRAD, col)
        else:
            comm(PAIR, end)

    small_in = small if not direct else refs[2].at[0]
    small_in[...] = small_a[...]
    ones = jnp.ones((8, rows_all), BF)
    for t in range(2):
        sums = dot(ones, g_mix[t])
        for col in range(3):
            at = slice(384 * t + 128 * col, 384 * t + 128 * (col + 1))
            small_in[17:18, at] = sums[0:1, 384 * col : 384 * col + 128]
            small_in[18:19, at] = sums[0:1, 384 * col + 256 : 384 * col + 384]
        at = slice(384 * t, 384 * (t + 1))
        small_in[19:20, at] = head_sum[t, 0:1, :] / affine[t, 1:2, 768:1152]
    if direct:
        little = Small(small, *refs[2:7])
        little.step()
    comm(SUMS)
    have(QKV_W)

    def resid_load(i):
        rows = pl.ds(i * ROW_BLOCK, ROW_BLOCK)
        return pltpu.make_async_copy(hbm_in[G_RESID].at[rows], resid.at[i % 2], resid_sem.at[i])

    def out_copy(i):
        rows = pl.ds(i * ROW_BLOCK, ROW_BLOCK)
        return pltpu.make_async_copy(grads_out.at[i % 2], tokens_grad.at[rows], out_sem.at[i])

    resid_load(0).start()
    for i in range(blocks):
        if i + 1 < blocks:
            resid_load(i + 1).start()
        resid_load(i).wait()
        if i >= 2:
            out_copy(i - 2).wait()
        rows = slice(i * ROW_BLOCK, (i + 1) * ROW_BLOCK)
        grads_out[i % 2] = resid[i % 2] + (
            dot(g_mix[0, rows, :], held[QKV_W][0], NT) + dot(g_mix[1, rows, :], held[QKV_W][1], NT)
        )
        out_copy(i).start()
        comm(ROWS, i)
    for i in range(max(0, blocks - 2), blocks):
        out_copy(i).wait()
    if direct:
        little.finish()
        scatter.finish()


HELD = (G_ATTN, CONTEXTS, G_FFN_T, NORMED_T, OUT_W, MIX, TOKENS, QKV_W)
LOADED = HELD + (ACTIV, G_PRE, G_RESID)


def backward_call(direct, affine, marks, lse, small_a, arrays):
    rows = arrays[TOKENS].shape[0]
    seqs = rows // SEQ_LEN
    blocks = rows // ROW_BLOCK
    scratch = [pltpu.VMEM(arrays[name].shape, arrays[name].dtype) for name in HELD]
    scratch += [
        pltpu.VMEM((3, rows, 768), BF),
        pltpu.VMEM((2, ROW_BLOCK, D), F32),
        pltpu.VMEM((2, ROW_BLOCK, D), F32),
        pltpu.VMEM((seqs, SEQ_LEN, SEQ_LEN), F32),
        pltpu.VMEM((2, rows, 384), BF),
        pltpu.VMEM((2, rows, 1152), BF),
        pltpu.VMEM((2, 8, 384), F32),
        pltpu.SemaphoreType.DMA((len(HELD),)),
        pltpu.SemaphoreType.DMA((9,)),
        pltpu.SemaphoreType.DMA((8,)),
        pltpu.SemaphoreType.DMA((blocks,)),
        pltpu.SemaphoreType.DMA((blocks,)),
    ]
    if direct:
        scratch += Scatter.scratch((768,) * 4 + (384,)) + Scatter.semaphores(SCATTER_CHUNKS)
        scratch += Small.scratch()
        extra = dict(collective_id=2, has_side_effects=True)
        grads = [jax.ShapeDtypeStruct((3, 48, 384), F32)]
        grads += [jax.ShapeDtypeStruct((48, w), F32) for w in WIDTHS[1:]]
    else:
        extra = {}
        grads = [jax.ShapeDtypeStruct((2, D, w), BF) for w in WIDTHS]
    tokens_grad, *grads, small = pl.pallas_call(
        functools.partial(backward_kernel, direct),
        out_shape=[
            jax.ShapeDtypeStruct((rows, D), F32),
            *grads,
            jax.ShapeDtypeStruct((SMALL_ROWS, D), F32),
        ],
        in_specs=vmem(4) + hbm(len(LOADED)),
        out_specs=hbm(1) + vmem(5),
        scratch_shapes=scratch,
        compiler_params=pltpu.CompilerParams(vmem_limit_bytes=VMEM_BYTES, **extra),
        name="backward",
    )(affine, marks, lse, small_a, *[arrays[name] for name in LOADED])
    return tokens_grad, grads, small


def finish_kernel(tokens_all, *refs):
    refs, moved = refs[:14] + refs[16:33], (refs[14:16], refs[33:35])
    for src, dst in zip(*moved):
        dst[...] = src[...]

    @pl.when(pl.program_id(0) == 0)
    def _():
        finish_small(tokens_all, *refs)


def finish_small(tokens_all, *refs):
    logits, noises = refs[:4], refs[4:8]
    scales, small = refs[8:10]
    grads, refs = refs[10:14], refs[14:]
    outs, refs = refs[:4], refs[4:]
    loss, qkv_b, out_b, up_b, down_b, gain1, shift1, gain2, shift2 = refs[:9]
    head, unit, width, layer = refs[9:]
    for src, dst in zip(grads, outs):
        dst[...] = src[...]
    zh, zu, zw, zl = (gate(flat_row(n), flat_row(v)) for n, v in zip(noises, logits))
    slope = lambda z: z * (1.0 - z) * 1.5

    def row(k):
        return small[k : k + 1, :]

    def put(ref, value):
        ref[...] = value.reshape(ref.shape)

    put(loss, jnp.sum(row(8), axis=1, keepdims=True) * (0.5 / tokens_all))
    qkv_b[...] = small[17:19, :]
    put(out_b, row(0) * scales[1:2, :])
    put(down_b, row(2) * scales[5:6, :])
    for k, ref in ((4, gain1), (5, shift1), (6, gain2), (7, shift2)):
        put(ref, row(k))
    put(up_b, jnp.concatenate([row(9 + j) for j in range(4)], axis=1))
    put(unit, jnp.concatenate([row(13 + j) for j in range(4)], axis=1) * slope(zu))
    put(width, (row(1) * zl[:, 0:1] + row(3) * zl[:, 1:2]) * slope(zw))
    at = lax.broadcasted_iota(jnp.int32, (1, 2), 1)
    first = jnp.sum(row(1) * zw, axis=1, keepdims=True)
    second = jnp.sum(row(3) * zw, axis=1, keepdims=True)
    put(layer, jnp.where(at == 0, first, second) * slope(zl))
    at = lax.broadcasted_iota(jnp.int32, (1, HEADS), 1)
    feature = lax.broadcasted_iota(jnp.int32, (1, D), 1) // HEAD_DIM
    total = jnp.zeros((1, HEADS), F32)
    for h in range(HEADS):
        mine = jnp.sum(jnp.where(feature == h, row(19), 0.0), axis=1, keepdims=True)
        total = jnp.where(at == h, mine, total)
    put(head, total * slope(zh))


def finish_call(tokens_all, raw, vec, small, grads, results):
    sizes = [1, 0, D, FF, D, D, D, D, D, HEADS, FF, D, 2]
    shapes = [jax.ShapeDtypeStruct(g.shape, F32) for g in grads]
    shapes += [jax.ShapeDtypeStruct((n,) if n else (2, D), F32) for n in sizes]
    by_rows = pl.BlockSpec((ROW_BLOCK, D), lambda i: (i, 0))

    def fixed(arrays):
        return [pl.BlockSpec(v.shape, lambda i, n=len(v.shape): (0,) * n) for v in arrays]

    ins = [*raw[LOGITS:], vec, small, *grads]
    return pl.pallas_call(
        functools.partial(finish_kernel, tokens_all),
        grid=(results[0].shape[0] // ROW_BLOCK,),
        out_shape=shapes + [jax.ShapeDtypeStruct(v.shape, v.dtype) for v in results],
        in_specs=fixed(ins) + [by_rows] * 2,
        out_specs=fixed(shapes) + [by_rows] * 2,
        name="finish",
    )(*ins, *results)


GATHER_CHUNKS = (
    (0, 0, 384, 0),
    (0, 384, 384, 0),
    (0, 768, 384, 0),
    (2, 0, 768, 0),
    (2, 768, 768, 0),
    (3, 0, 768, 0),
    (3, 768, 768, 0),
    (1, 0, 384, 1),
)
SCATTER_CHUNKS = (
    (1, 0, 384, 4, 0),
    (3, 0, 768, 0, 0),
    (3, 768, 768, 1, 0),
    (2, 0, 768, 2, 0),
    (2, 768, 768, 3, 0),
    (0, 0, 384, 4, 0),
    (0, 128, 384, 0, 0),
    (0, 256, 384, 0, 384),
)


def body(direct, tokens, teacher, segments, qkv_weight, qkv_bias, out_weight, out_bias, *args):
    up_weight, up_bias, down_weight, *args = args
    raw = (qkv_bias, out_bias, up_bias, *args)
    kinds = jnp.transpose(qkv_weight, (1, 0, 2))
    weights = [kinds, out_weight, up_weight, down_weight]
    if not direct:
        weights[0] = qkv_weight.reshape(-1, 1152)
        weights = [
            lax.all_gather(lax.all_gather(s, "dp", axis=0, tiled=True), "tensor", axis=0)
            for s in weights
        ]
    lse, affine, vec, small_a, arrays = forward_call(
        direct, tokens, teacher, segments, raw, weights
    )
    tokens_grad, grads, small = backward_call(direct, affine, segments, lse, small_a, arrays)
    if not direct:
        grads = [
            lax.psum_scatter(
                lax.psum_scatter(g, "tensor", scatter_dimension=0),
                "dp",
                scatter_dimension=0,
                tiled=True,
            ).astype(F32)
            for g in grads
        ]
        grads[0] = jnp.transpose(grads[0].reshape(-1, 3, 384), (1, 0, 2))
        small = lax.psum(small, ("dp", "tensor"))
    all_tokens = tokens.shape[0] * lax.axis_size("dp") * lax.axis_size("tensor")
    outs = finish_call(
        all_tokens, raw, vec, small, grads, (arrays[ACTIVATIONS], tokens_grad)
    )
    *outs, activations, tokens_grad = outs
    qkv_grad, out_grad, up_grad, down_grad, loss, qkv_b, out_b, up_b, down_b = outs[:9]
    return (
        activations,
        loss.reshape(()),
        tokens_grad,
        jnp.transpose(qkv_grad, (1, 0, 2)),
        qkv_b,
        out_grad,
        out_b,
        up_grad,
        up_b,
        down_grad,
        down_b,
        *outs[9:],
    )


def solution(mesh):
    rows, split, whole = P(("dp", "tensor"), None), P("dp", "tensor"), P()
    cube = P("dp", None, "tensor")
    in_specs = (rows, rows, rows, cube, whole, split, whole, split, whole, split) + (whole,) * 13
    out_specs = (
        rows,
        whole,
        rows,
        cube,
        whole,
        split,
        whole,
        split,
        whole,
        split,
    ) + (whole,) * 9
    direct = mesh.shape["dp"] == 16 and mesh.shape["tensor"] == 2
    return jax.shard_map(
        functools.partial(body, direct),
        mesh=mesh,
        in_specs=in_specs,
        out_specs=out_specs,
        check_vma=False,
    )
```

```python
import functools

import jax
import jax.numpy as jnp
from jax import lax
from jax.experimental import pallas as pl
from jax.experimental.pallas import tpu as pltpu
from jax.sharding import PartitionSpec as P

D = 768
HEADS = 12
HEAD_DIM = 64
FF = 3072
SEQ_LEN = 512
BETA = 2.0 / 3.0
EPS = 1e-12
NEG = -1e30
BF = jnp.bfloat16
F32 = jnp.float32
MESH = pl.DeviceIdType.MESH
VMEM_BYTES = 60 * 1024 * 1024
WIDTHS = (1152, 384, 1536, 1536)
ROW_BLOCK = 256
SMALL_ROWS = 24
NT = (((1,), (1,)), ((), ()))
TN = (((0,), (0,)), ((), ()))
NN = (((1,), (0,)), ((), ()))


def dot(left, right, dims=NN):
    return lax.dot_general(left, right, dims, preferred_element_type=F32)


def vmem(n=1):
    return [pl.BlockSpec(memory_space=pltpu.VMEM)] * n


def hbm(n=1):
    return [pl.BlockSpec(memory_space=pl.ANY)] * n


def coords():
    dp = lax.axis_index("dp")
    return dp // 4, lax.rem(dp // 2, 2), lax.axis_index("tensor"), lax.rem(dp, 2)


def place(z, x, y, c):
    return ((z * 2 + x) * 2 + c, y)


def partners():
    z, x, y, c = coords()
    along = [(lax.rem(z + k, 4), x, y, c) for k in (1, 2, 3)]
    return along + [(z, 1 - x, y, c), (z, x, 1 - y, c), (z, x, y, 1 - c)]


def greet():
    barrier = pltpu.get_barrier_semaphore()
    for partner in partners():
        pl.semaphore_signal(barrier, inc=1, device_id=place(*partner), device_id_type=MESH)


def met():
    pl.semaphore_wait(pltpu.get_barrier_semaphore(), 6)


class Gather:
    COPIES = 12

    def __init__(self, chunks, ins, outs, local_sem, send_sem, recv_sem):
        self.chunks, self.ins, self.outs = chunks, ins, outs
        self.local_sem, self.send_sem, self.recv_sem = local_sem, send_sem, recv_sem
        self.kept = {}
        self.started = []
        self.locals = {}

    def send(self, chunk, slot, src, dst, target):
        copy = pltpu.make_async_remote_copy(
            src_ref=src,
            dst_ref=dst,
            send_sem=self.send_sem.at[chunk, slot],
            recv_sem=self.recv_sem.at[chunk, slot],
            device_id=place(*target),
            device_id_type=MESH,
        )
        copy.start()
        self.started.append(copy)
        self.kept[chunk, slot] = copy

    def arrived(self, chunk, *slots):
        for slot in slots:
            self.kept[chunk, slot].wait_recv()

    def source(self, chunk):
        which, start, size, _ = self.chunks[chunk]
        if which == 0:
            return self.ins[0].at[start // size]
        return self.ins[which].at[:, pl.ds(start, size)]

    def target(self, chunk):
        which, start, size, _ = self.chunks[chunk]
        z, x, y, c = coords()
        return self.outs[which].at[y, z, x, c, :, pl.ds(start, size)]

    def own(self):
        for i in range(len(self.chunks)):
            copy = pltpu.make_async_copy(self.source(i), self.target(i), self.local_sem.at[i])
            copy.start()
            self.locals[i] = copy

    def phase(self, chunk, phase):
        z, x, y, c = coords()
        across, beside, core = (z, 1 - x, y, c), (z, x, 1 - y, c), (z, x, y, 1 - c)
        which, start, size, flat_first = self.chunks[chunk]
        cols = pl.ds(start, size)
        out = self.outs[which]

        def pass_on(slot, view, target):
            self.send(chunk, slot, view, view, target)

        if flat_first:
            if phase == 0:
                self.send(chunk, 0, self.source(chunk), self.target(chunk), across)
                self.send(chunk, 1, self.source(chunk), self.target(chunk), beside)
            elif phase == 1:
                self.arrived(chunk, 0, 1)
                t, v = y + c * (1 - 2 * y), 1 - x + c * (2 * x - 1)
                pass_on(2, out.at[t, z, v, c, :, cols], (z, 1 - v, 1 - t, c))
            elif phase == 2:
                self.locals[chunk].wait()
                self.arrived(chunk, 2)
                for k in range(3):
                    to = lax.rem(z + k + 1, 4)
                    pass_on(3 + k, out.at[:, z, :, c, :, cols], (to, x, y, c))
            elif phase == 3:
                self.arrived(chunk, 3, 4, 5)
                pass_on(6, out.at[:, :, :, c, :, cols], core)
            else:
                self.arrived(chunk, 6)
            return
        if phase == 0:
            for k in range(3):
                self.send(
                    chunk,
                    k,
                    self.source(chunk),
                    self.target(chunk),
                    (lax.rem(z + k + 1, 4), x, y, c),
                )
        elif phase == 1:
            self.locals[chunk].wait()
            self.arrived(chunk, 0, 1, 2)
            pass_on(3, out.at[y, 0:2, x, c, :, cols], across)
            pass_on(4, out.at[y, 2:4, x, c, :, cols], beside)
            pass_on(7, out.at[y, :, x, c, :, cols], core)
        elif phase == 2:
            self.arrived(chunk, 3)
            pass_on(5, out.at[y, 0:2, :, c, :, cols], beside)
            self.arrived(chunk, 4)
            pass_on(6, out.at[:, 2:4, x, c, :, cols], across)
            pass_on(8, out.at[y, 0:2, 1 - x, c, :, cols], core)
            pass_on(9, out.at[1 - y, 2:4, x, c, :, cols], core)
        elif phase == 3:
            self.arrived(chunk, 5)
            pass_on(10, out.at[1 - y, 0:2, :, c, :, cols], core)
            self.arrived(chunk, 6)
            pass_on(11, out.at[:, 2:4, 1 - x, c, :, cols], core)
        else:
            self.arrived(chunk, 7, 8, 9, 10, 11)

    def finish(self):
        for copy in self.started:
            copy.wait_send()


class Scatter:
    COPIES = 8

    def __init__(self, chunks, outs, bufs, send_sem, recv_sem):
        self.chunks, self.outs, self.bufs = chunks, outs, bufs
        self.send_sem, self.recv_sem = send_sem, recv_sem
        self.kept = {}
        self.started = {}

    def send(self, chunk, slot, src, dst, target):
        copy = pltpu.make_async_remote_copy(
            src_ref=src,
            dst_ref=dst,
            send_sem=self.send_sem.at[chunk, slot],
            recv_sem=self.recv_sem.at[chunk, slot],
            device_id=place(*target),
            device_id_type=MESH,
        )
        copy.start()
        self.started.setdefault(chunk, []).append(copy)
        self.kept[chunk, slot] = copy

    def arrived(self, chunk, *slots):
        for slot in slots:
            self.kept[chunk, slot].wait_recv()

    def release(self, chunk):
        for copy in self.started.pop(chunk, []):
            copy.wait_send()

    def views(self, chunk):
        _, _, size, at, lane = self.chunks[chunk]
        return tuple(
            ref.at[(slice(None),) * (len(ref.shape) - 1) + (pl.ds(lane, size),)]
            for ref in self.bufs[at]
        )

    def fill(self, chunk, half, value):
        c = coords()[3]
        both = self.views(chunk)[0]
        for i in range(16):
            z, x, k = i // 4, (i // 2) % 2, i % 2
            side = lax.rem(c + k, 2)
            both[side, half, z, x] = value[48 * i : 48 * (i + 1), :].astype(BF)

    def phase(self, chunk, phase):
        z, x, y, c = coords()
        across, beside, core = (z, 1 - x, y, c), (z, x, 1 - y, c), (z, x, y, 1 - c)
        both, first, low_a, low_b, last_a, last_b, last = self.views(chunk)
        sums = both.at[0]

        def add(left, right):
            left[...] = (left[...].astype(F32) + right[...].astype(F32)).astype(BF)

        if phase == 0:
            self.send(chunk, 0, both.at[1], first, core)
        elif phase == 1:
            self.arrived(chunk, 0)

            @pl.loop(0, 16)
            def _(i):
                at = (i // 8, lax.rem(i // 2, 4), lax.rem(i, 2))
                add(sums.at[at], first.at[at])

            self.send(chunk, 1, sums.at[1 - y, 0:2], low_a, beside)
            self.send(chunk, 2, sums.at[:, 2:4, 1 - x], low_b, across)
        elif phase == 2:
            self.arrived(chunk, 1)

            @pl.loop(0, 4)
            def _(i):
                k, v = i // 2, lax.rem(i, 2)
                add(sums.at[y, k, v], low_a.at[k, v])

            self.send(chunk, 3, sums.at[y, 0:2, 1 - x], last_a, across)
            self.arrived(chunk, 2)

            @pl.loop(0, 4)
            def _(i):
                t, k = i // 2, lax.rem(i, 2)
                add(sums.at[t, k + 2, x], low_b.at[t, k])

            self.send(chunk, 4, sums.at[1 - y, 2:4, x], last_b, beside)
        elif phase == 3:
            self.arrived(chunk, 3, 4)

            @pl.loop(0, 2)
            def _(k):
                add(sums.at[y, k, x], last_a.at[k])
                add(sums.at[y, k + 2, x], last_b.at[k])

            for k in range(3):
                to = lax.rem(z + k + 1, 4)
                self.send(chunk, 5 + k, sums.at[y, to, x], last.at[k], (to, x, y, c))
        else:
            self.arrived(chunk, 5, 6, 7)
            total = sums[y, z, x].astype(F32)
            for k in range(3):
                total = total + last[k].astype(F32)
            which, start, size = self.chunks[chunk][:3]
            if which == 0:
                for kind in range(3):
                    part = total[:, 128 * kind : 128 * (kind + 1)]
                    self.outs[0][kind, :, pl.ds(start, 128)] = part
            else:
                self.outs[which][:, pl.ds(start, size)] = total

    def finish(self):
        for chunk in list(self.started):
            self.release(chunk)

    @staticmethod
    def scratch(sizes):
        shapes = []
        for n in sizes:
            shapes += [
                pltpu.VMEM((2, 2, 4, 2, 48, n), BF),
                pltpu.VMEM((2, 4, 2, 48, n), BF),
                pltpu.VMEM((2, 2, 48, n), BF),
                pltpu.VMEM((2, 2, 48, n), BF),
                pltpu.VMEM((2, 48, n), BF),
                pltpu.VMEM((2, 48, n), BF),
                pltpu.VMEM((3, 48, n), BF),
            ]
        return shapes

    @staticmethod
    def semaphores(chunks):
        n = len(chunks)
        return [
            pltpu.SemaphoreType.DMA((n, Scatter.COPIES)),
            pltpu.SemaphoreType.DMA((n, Scatter.COPIES)),
        ]


class Small:
    def __init__(self, out, own, got, lines, send_sem, recv_sem):
        self.out, self.own, self.got, self.lines = out, own, got, lines
        self.send_sem, self.recv_sem = send_sem, recv_sem
        self.pending = []
        self.step_at = 0

    def send(self, slot, src, dst, target):
        copy = pltpu.make_async_remote_copy(
            src_ref=src,
            dst_ref=dst,
            send_sem=self.send_sem.at[slot],
            recv_sem=self.recv_sem.at[slot],
            device_id=place(*target),
            device_id_type=MESH,
        )
        copy.start()
        self.pending.append(copy)

    def step(self):
        z, x, y, c = coords()
        nearby = ((z, x, y, 1 - c), (z, 1 - x, y, c), (z, x, 1 - y, c))
        at = self.step_at
        if at > 4:
            return
        self.step_at += 1
        for copy in self.pending:
            copy.wait()
        self.pending = []
        if 1 <= at <= 3:
            self.own[at] = self.own[at - 1] + self.got[at - 1]
        if at < 3:
            self.send(at, self.own.at[at], self.got.at[at], nearby[at])
        elif at == 3:
            self.lines[z] = self.own[3]
            for k in range(3):
                to = (lax.rem(z + k + 1, 4), x, y, c)
                self.send(3 + k, self.own.at[3], self.lines.at[z], to)
        else:
            self.out[...] = (self.lines[0] + self.lines[1]) + (self.lines[2] + self.lines[3])

    def finish(self):
        while self.step_at <= 4:
            self.step()

    @staticmethod
    def scratch():
        return [
            pltpu.VMEM((4, SMALL_ROWS, D), F32),
            pltpu.VMEM((3, SMALL_ROWS, D), F32),
            pltpu.VMEM((4, SMALL_ROWS, D), F32),
            pltpu.SemaphoreType.DMA((6,)),
            pltpu.SemaphoreType.DMA((6,)),
        ]


def head_masks():
    lane = lax.broadcasted_iota(jnp.int32, (SEQ_LEN, 128), 1)
    return lane < HEAD_DIM


def pair_at(i):
    seq, pair = i // 6, lax.rem(i, 6)
    half, col = pair // 3, lax.rem(pair, 3)
    return seq, half, col, pl.ds(pl.multiple_of(seq * SEQ_LEN, SEQ_LEN), SEQ_LEN)


def lanes(col, base):
    return pl.ds(pl.multiple_of(base + col * 128, 128), 128)


def mask_into(bias, marks):
    for s in range(bias.shape[0]):
        item = lax.broadcasted_iota(jnp.int32, (16, SEQ_LEN), 0)
        hot = jnp.where(marks[s : s + 1, :] == item, 1.0, 0.0).astype(BF)
        bias[s] = (dot(hot, hot, TN) - 1.0) * -NEG


def gate(noise, logit):
    return jax.nn.sigmoid((jnp.log(noise) - jnp.log1p(-noise) + logit) * (1.0 / BETA))


def flat_row(ref):
    return ref[...].reshape(1, ref.shape[0])


def over_heads(values):
    head = lax.broadcasted_iota(jnp.int32, (1, D), 1) // HEAD_DIM
    out = jnp.zeros((1, D), F32)
    for h in range(HEADS):
        out = jnp.where(head == h, values[:, h : h + 1], out)
    return out


def prepare(raw, affine, vec, uvec):
    zh = over_heads(gate_of(raw, HEAD))
    zw = gate_of(raw, WIDTH)
    zl = gate_of(raw, LAYER)
    for t in range(2):
        cols = slice(384 * t, 384 * (t + 1))
        affine[t, 0:1, 0:384] = raw[QKV_BIAS][0:1, cols]
        affine[t, 0:1, 384:768] = jnp.zeros((1, 384), F32)
        affine[t, 0:1, 768:1152] = raw[QKV_BIAS][1:2, cols]
        affine[t, 1:2, 0:384] = jnp.full((1, 384), HEAD_DIM**-0.5, F32)
        affine[t, 1:2, 384:768] = jnp.ones((1, 384), F32)
        affine[t, 1:2, 768:1152] = zh[:, cols]
    for i, name in enumerate(VEC):
        vec[i : i + 1, :] = zl[:, i // 4 : i // 4 + 1] * zw if name is None else flat_row(raw[name])
    uvec[0:1, :] = flat_row(raw[UP_BIAS])
    uvec[1:2, :] = gate_of(raw, UNIT)


QKV_BIAS, OUT_BIAS, UP_BIAS, DOWN_BIAS, GAIN1, SHIFT1, GAIN2, SHIFT2 = range(8)
LOGITS, NOISES = 8, 12
HEAD, UNIT, WIDTH, LAYER = range(4)
PREP = 16
VEC = (OUT_BIAS, None, GAIN1, SHIFT1, DOWN_BIAS, None, GAIN2, SHIFT2)


def gate_of(raw, kind):
    return gate(flat_row(raw[NOISES + kind]), flat_row(raw[LOGITS + kind]))


def project(i, tokens, weight, affine, mix):
    rows = pl.ds(pl.multiple_of(i * ROW_BLOCK, ROW_BLOCK), ROW_BLOCK)
    for t in range(2):
        mixed = dot(tokens[rows, :], weight(t))
        mix[t, rows, :] = ((mixed + affine[t, 0:1, :]) * affine[t, 1:2, :]).astype(BF)


def attend(i, mix, bias, context, lse):
    left = head_masks()
    seq, t, col, rows = pair_at(i)
    query = mix[t, rows, lanes(col, 0)]
    keys = mix[t, rows, lanes(col, 384)]
    values = mix[t, rows, lanes(col, 768)]
    parts = []
    for h in range(2):
        mine = jnp.where(left if h == 0 else ~left, query, 0)
        scores = dot(mine, keys, NT) + bias[seq]
        top = jnp.max(scores, axis=1, keepdims=True)
        expo = jnp.exp(scores - top)
        total = jnp.sum(expo, axis=1, keepdims=True)
        probs = (expo * (1.0 / total)).astype(BF)
        parts.append(dot(probs, values))
        logsum = jnp.broadcast_to(top + jnp.log(total), (SEQ_LEN, 128))
        lse[i, h : h + 1, :] = jnp.transpose(logsum)[0:1, :]
    context[t, rows, lanes(col, 0)] = jnp.where(left, parts[0], parts[1]).astype(BF)


def attend_back(m, mix, bias, lse, g_context, affine, g_mix, head_sum):
    left = head_masks()
    seq, t, col = lax.rem(m, 2), lax.rem(m // 2, 2), m // 4
    i = seq * 6 + t * 3 + col
    rows = pl.ds(pl.multiple_of(seq * SEQ_LEN, SEQ_LEN), SEQ_LEN)
    query = mix[t, rows, lanes(col, 0)]
    keys = mix[t, rows, lanes(col, 384)]
    values = mix[t, rows, lanes(col, 768)]
    grad = g_context[t, rows, lanes(col, 0)]
    parts = []
    for h in range(2):
        side = left if h == 0 else ~left
        scores = dot(jnp.where(side, keys, 0), query, NT) + bias[seq]
        probs = jnp.exp(scores - lse[i, h : h + 1, :])
        g_probs = dot(jnp.where(side, values, 0), grad, NT)
        delta = jnp.sum(g_probs * probs, axis=0, keepdims=True)
        g_scores = (probs * (g_probs - delta)).astype(BF)
        parts.append(
            (
                dot(g_scores, keys, TN),
                dot(g_scores, query),
                dot(probs.astype(BF), grad),
            )
        )
    g_query, g_keys, g_values = (jnp.where(left, a, b) for a, b in zip(*parts))
    g_mix[t, rows, lanes(3 * col, 0)] = (g_query * HEAD_DIM**-0.5).astype(BF)
    g_mix[t, rows, lanes(3 * col, 128)] = g_keys.astype(BF)
    used = affine[t, 1:2, lanes(col, 768)]
    g_mix[t, rows, lanes(3 * col, 256)] = (g_values * used).astype(BF)
    used = jnp.sum(g_values * values.astype(F32), axis=0, keepdims=True)
    head_sum[t, 0:1, lanes(col, 0)] += used


def normalise(value):
    mean = jnp.mean(value, axis=1, keepdims=True)
    centred = value - mean
    var = jnp.mean(centred * centred, axis=1, keepdims=True)
    rstd = lax.rsqrt(var + EPS)
    return centred * rstd, rstd


def norm_back(grad, unit, rstd):
    mean = jnp.mean(grad, axis=1, keepdims=True)
    along = jnp.mean(grad * unit, axis=1, keepdims=True)
    return rstd * (grad - mean - unit * along)


def fold(value):
    return jnp.sum(value.reshape(value.shape[0] // 8, 8, value.shape[1]), axis=0)


START, PROJECT, PAIRS, UP = range(4)
ARRIVE = {
    (START, 0): ((0, 0), (1, 0), (7, 0), (7, 1), (0, 1), (1, 1), (2, 0), (3, 0), (0, 2), (1, 2), (2, 1), (4, 0), (3, 1), (5, 0), (0, 3), (1, 3), (2, 2), (0, 4), (1, 4), (3, 2), (4, 1), (6, 0), (2, 3), (2, 4)),
    (PROJECT, 0): ((5, 1), (7, 2)),
    (PAIRS, 1): ((4, 2),),
    (PAIRS, 4): ((3, 3), (6, 1)),
    (PAIRS, 6): ((5, 2),),
    (PAIRS, 9): ((3, 4),),
    (PAIRS, 11): ((7, 3), (6, 2), (7, 4), (4, 3), (4, 4)),
    (UP, 0): ((5, 3),),
    (UP, 1): ((5, 4), (6, 3)),
    (UP, 2): ((6, 4),),
}


def spans(direct, kind, count):
    begin = 0
    for i in range(count):
        if (direct and (kind, i) in ARRIVE) or i == count - 1:
            yield begin, i + 1
            begin = i + 1


def forward_kernel(direct, *refs):
    tokens, teacher, marks = refs[:3]
    raw = refs[3 : 3 + PREP]
    refs = refs[3 + PREP :]
    weights, refs = refs[:4], refs[4:]
    if direct:
        full, refs = refs[:2], refs[2:]
    lse, affine, vec, small = refs[:4]
    out = refs[4 : 4 + STREAMED]
    refs = refs[4 + STREAMED :]
    held, refs = refs[:4], refs[4:]
    mix, context, attn, bias, uvec, deriv, activ = refs[:7]
    normed_t, g_ffn_t, result_low, g_attn, sums, unit_sums = refs[7:13]
    keep_sem, load_sem, stream_sem = refs[13:16]
    refs = refs[16:]
    rows_all = tokens.shape[0]
    blocks = rows_all // ROW_BLOCK
    if direct:
        gather = Gather(GATHER_CHUNKS, weights, held, *refs)
        greet()
        gather.own()
        prepare(raw, affine, vec, uvec)
        met()
    else:
        loads = [pltpu.make_async_copy(*pair, load_sem.at[i]) for i, pair in enumerate(zip(weights, held))]
        for copy in loads:
            copy.start()
        prepare(raw, affine, vec, uvec)
        for copy in loads:
            copy.wait()
    mask_into(bias, marks)
    sums[...] = jnp.zeros_like(sums)
    unit_sums[...] = jnp.zeros_like(unit_sums)

    def weight(which, t):
        return held[which][t].reshape(D, WIDTHS[which])

    def comm(piece, i=0):
        if direct:
            for chunk, phase in ARRIVE.get((piece, i), ()):
                gather.phase(chunk, phase)

    kept = []

    def keep(src, dst):
        copy = pltpu.make_async_copy(src, dst, keep_sem.at[len(kept)])
        copy.start()
        kept.append(copy)

    def row_span(i):
        start = i * ROW_BLOCK
        return pl.ds(start if isinstance(i, int) else pl.multiple_of(start, ROW_BLOCK), ROW_BLOCK)

    def stream(name, i):
        rows = row_span(i)
        across = out[name].at[:, rows] if name in (NORMED_T, G_FFN_T) else out[name].at[rows]
        source = {
            ACTIVATIONS: result_low,
            G_ATTN: g_attn,
            G_RESID: attn,
            ACTIV: activ,
            G_PRE: activ,
        }
        if name in source:
            src = source[name].at[rows]
        else:
            src = (normed_t if name == NORMED_T else g_ffn_t).at[i]
        return pltpu.make_async_copy(src, across, stream_sem.at[name, i])

    comm(START)
    if direct:
        keep(held[0], full[0])
    for begin, end in spans(direct, PROJECT, blocks):

        @pl.loop(begin, end)
        def _(i):
            project(i, tokens, lambda t: weight(0, t), affine, mix)

        comm(PROJECT, end - 1)
    for begin, end in spans(direct, PAIRS, 12):

        @pl.loop(begin, end)
        def _(i):
            attend(i, mix, bias, context, lse)

        comm(PAIRS, end - 1)
    if direct:
        keep(held[1], full[1])
    keep(mix, out[MIX])
    keep(context, out[CONTEXTS])
    out_bias, scale1, gain1, shift1 = (vec[i : i + 1, :] for i in range(4))
    down_bias, scale2, gain2, shift2 = (vec[i : i + 1, :] for i in range(4, 8))

    def upward(i):
        rows = row_span(i)
        both = dot(context[0, rows, :], weight(1, 0), NT) + dot(context[1, rows, :], weight(1, 1), NT)
        attn[rows, :] = both
        unit1, _ = normalise(tokens[rows, :].astype(F32) + (both + out_bias) * scale1)
        normed_low = (unit1 * gain1 + shift1).astype(BF)
        normed_t[i] = jnp.transpose(normed_low)
        stream(NORMED_T, i).start()
        for t in range(2):
            flat = slice(1536 * t, 1536 * (t + 1))
            pre = dot(normed_low, weight(2, t)) + uvec[0:1, flat]
            gates = uvec[1:2, flat]
            phi = 0.5 + 0.5 * lax.erf(pre * (0.5**0.5))
            pdf = jnp.exp(pre * pre * -0.5) * ((2.0 * jnp.pi) ** -0.5)
            deriv[rows, flat] = (phi + pre * pdf) * gates
            activ[rows, flat] = (pre * phi * gates).astype(BF)
        stream(ACTIV, i).start()

    if direct:
        for i in range(blocks):
            upward(i)
            comm(UP, i)
    else:
        pl.loop(0, blocks)(upward)

    @pl.loop(0, blocks)
    def _(i):
        rows = row_span(i)
        attn_b = attn[rows, :] + out_bias
        unit1, rstd1 = normalise(tokens[rows, :].astype(F32) + attn_b * scale1)
        normed = unit1 * gain1 + shift1
        ffn_b = (
            dot(activ[rows, 0:1536], weight(3, 0), NT) + dot(activ[rows, 1536:3072], weight(3, 1), NT)
        ) + down_bias
        unit2, rstd2 = normalise(normed + ffn_b * scale2)
        result = unit2 * gain2 + shift2
        result_low[rows, :] = result.astype(BF)
        stream(ACTIVATIONS, i).start()
        diff = result - teacher[rows, :].astype(F32)
        g_value2 = norm_back(diff * gain2, unit2, rstd2)
        g_ffn_low = (g_value2 * scale2).astype(BF)
        g_ffn_t[i] = jnp.transpose(g_ffn_low)
        stream(G_FFN_T, i).start()
        sums[2] += fold(g_value2)
        sums[3] += fold(g_value2 * ffn_b)
        sums[6] += fold(diff * unit2)
        sums[7] += fold(diff)
        sums[8] += fold(diff * diff)
        ones = jnp.ones((8, ROW_BLOCK), BF)
        stream(ACTIV, i).wait()
        g_normed = g_value2
        for t in range(2):
            flat = slice(1536 * t, 1536 * (t + 1))
            g_activ = dot(g_ffn_low, weight(3, t))
            unit_sums[0, :, flat] += fold(g_activ * activ[rows, flat].astype(F32))
            grad = (g_activ * deriv[rows, flat]).astype(BF)
            activ[rows, flat] = grad
            unit_sums[1, :, flat] += dot(ones, grad)
            g_normed = g_normed + dot(grad, weight(2, t), NT)
        stream(G_PRE, i).start()
        g_value1 = norm_back(g_normed * gain1, unit1, rstd1)
        attn[rows, :] = g_value1
        stream(G_RESID, i).start()
        g_attn[rows, :] = (g_value1 * scale1).astype(BF)
        stream(G_ATTN, i).start()
        sums[0] += fold(g_value1)
        sums[1] += fold(g_value1 * attn_b)
        sums[4] += fold(g_normed * unit1)
        sums[5] += fold(g_normed)

    small[...] = jnp.zeros_like(small)
    for k in range(9):
        small[k : k + 1, :] = jnp.sum(sums[k], axis=0, keepdims=True)
    for j in range(4):
        cols = slice(768 * j, 768 * (j + 1))
        small[9 + j : 10 + j, :] = unit_sums[1, 0:1, cols]
        total = jnp.sum(unit_sums[0, :, cols], axis=0, keepdims=True)
        small[13 + j : 14 + j, :] = total / uvec[1:2, cols]
    for name in range(2, STREAMED):
        for i in range(blocks):
            if name != ACTIV:
                stream(name, i).wait()
    for copy in kept:
        copy.wait()
    if direct:
        gather.finish()


MIX, CONTEXTS, ACTIVATIONS, G_ATTN, G_RESID, ACTIV, G_PRE, NORMED_T, G_FFN_T = range(9)
STREAMED = 9
QKV_W, OUT_W, TOKENS = range(9, 12)


def forward_call(direct, tokens, teacher, marks, raw, weights):
    rows = tokens.shape[0]
    seqs = rows // SEQ_LEN
    blocks = rows // ROW_BLOCK
    n = len(GATHER_CHUNKS)
    full = [jax.ShapeDtypeStruct((2, 4, 2, 2, 48, w), BF) for w in WIDTHS]
    shapes = [
        jax.ShapeDtypeStruct((6 * seqs, 8, SEQ_LEN), F32),
        jax.ShapeDtypeStruct((2, 8, 1152), F32),
        jax.ShapeDtypeStruct((8, D), F32),
        jax.ShapeDtypeStruct((SMALL_ROWS, D), F32),
    ]
    streamed = [
        jax.ShapeDtypeStruct((2, rows, 1152), BF),
        jax.ShapeDtypeStruct((2, rows, 384), BF),
        jax.ShapeDtypeStruct((rows, D), BF),
        jax.ShapeDtypeStruct((rows, D), BF),
        jax.ShapeDtypeStruct((rows, D), F32),
        jax.ShapeDtypeStruct((rows, FF), BF),
        jax.ShapeDtypeStruct((rows, FF), BF),
        jax.ShapeDtypeStruct((D, rows), BF),
        jax.ShapeDtypeStruct((D, rows), BF),
    ]
    scratch = [pltpu.VMEM(f.shape, BF) for f in full]
    scratch += [
        pltpu.VMEM((2, rows, 1152), BF),
        pltpu.VMEM((2, rows, 384), BF),
        pltpu.VMEM((rows, D), F32),
        pltpu.VMEM((seqs, SEQ_LEN, SEQ_LEN), F32),
        pltpu.VMEM((8, FF), F32),
        pltpu.VMEM((rows, FF), F32),
        pltpu.VMEM((rows, FF), BF),
        pltpu.VMEM((blocks, D, ROW_BLOCK), BF),
        pltpu.VMEM((blocks, D, ROW_BLOCK), BF),
        pltpu.VMEM((rows, D), BF),
        pltpu.VMEM((rows, D), BF),
        pltpu.VMEM((9, 8, D), F32),
        pltpu.VMEM((2, 8, FF), F32),
        pltpu.SemaphoreType.DMA((4,)),
        pltpu.SemaphoreType.DMA((4,)),
        pltpu.SemaphoreType.DMA((STREAMED, blocks)),
    ]
    extra = {}
    if direct:
        scratch += [
            pltpu.SemaphoreType.DMA((n,)),
            pltpu.SemaphoreType.DMA((n, Gather.COPIES)),
            pltpu.SemaphoreType.DMA((n, Gather.COPIES)),
        ]
        extra = dict(collective_id=1, has_side_effects=True)
    else:
        weights = [w.reshape(f.shape) for w, f in zip(weights, full)]
    outs = pl.pallas_call(
        functools.partial(forward_kernel, direct),
        out_shape=(full[:2] if direct else []) + shapes + streamed,
        in_specs=vmem(3 + PREP) + (vmem(4) if direct else hbm(4)),
        out_specs=(hbm(2) if direct else []) + vmem(len(shapes)) + hbm(len(streamed)),
        scratch_shapes=scratch,
        compiler_params=pltpu.CompilerParams(vmem_limit_bytes=VMEM_BYTES, **extra),
        name="forward",
    )(tokens, teacher, marks, *raw, *weights)
    if direct:
        weights, outs = outs[:2], outs[2:]
    weights = [w.reshape(2, D, w.shape[-1]) for w in weights[:2]]
    lse, affine, vec, small = outs[:4]
    arrays = [*outs[4:], weights[0], weights[1], tokens]
    return lse, affine, vec, small, arrays


OUT, FEED, CONTEXT, PAIR, QGRAD, SUMS, ROWS = range(7)
LITTLE = None
FOLLOW = {
    (OUT, 0): ((0, 0),),
    (FEED, 1): ((1, 0),),
    (FEED, 2): ((0, 1),),
    (FEED, 3): ((2, 0),),
    (FEED, 4): ((1, 1),),
    (FEED, 5): ((0, 2), (2, 1), (3, 0)),
    (FEED, 7): ((4, 0),),
    (PAIR, 0): ((1, 2), (0, 3), (3, 1)),
    (PAIR, 3): ((0, 4), (2, 2), (4, 1), (1, 3)),
    (QGRAD, 0): ((5, 0),),
    (PAIR, 5): ((3, 2), (5, 1)),
    (PAIR, 6): ((1, 4), (2, 3)),
    (QGRAD, 1): ((6, 0),),
    (PAIR, 8): ((4, 2),),
    (PAIR, 9): ((3, 3), (2, 4), (6, 1)),
    (PAIR, 10): ((5, 2),),
    (QGRAD, 2): ((4, 3), (7, 0)),
    (ROWS, 0): ((3, 4), (6, 2)),
    (ROWS, 1): ((5, 3), LITTLE, (7, 1)),
    (ROWS, 3): (
        ((6, 3), (4, 4), LITTLE, (7, 2), (5, 4), LITTLE, (7, 3), (6, 4), (7, 4), LITTLE)
    ),
}


def backward_kernel(direct, *refs):
    affine, marks, lse, small_a = refs[:4]
    hbm_in, refs = dict(zip(LOADED, refs[4 : 4 + len(LOADED)])), refs[4 + len(LOADED) :]
    tokens_grad, refs = refs[0], refs[1:]
    outs, refs = refs[:4], refs[4:]
    small, refs = refs[0], refs[1:]
    held = dict(zip(HELD, refs[: len(HELD)]))
    refs = refs[len(HELD) :]
    ring, resid, grads_out, bias, g_context, g_mix, head_sum = refs[:7]
    load_sem, qkv_sem, ring_sem, resid_sem, out_sem = refs[7:12]
    refs = refs[12:]
    rows_all = bias.shape[0] * SEQ_LEN
    blocks = rows_all // ROW_BLOCK
    loads = {}
    ring_loads = {}

    def load(*names):
        for name in names:
            i = HELD.index(name)
            loads[name] = []
            if name == QKV_W:
                for k in range(9):
                    kind, col = k % 3, k // 3
                    src = hbm_in[name].at[:, :, pl.ds(384 * kind + 128 * col, 128)]
                    dst = held[name].at[:, :, pl.ds(128 * k, 128)]
                    loads[name].append(pltpu.make_async_copy(src, dst, qkv_sem.at[k]))
            else:
                copy = pltpu.make_async_copy(hbm_in[name], held[name], load_sem.at[i])
                loads[name].append(copy)
            for copy in loads[name]:
                copy.start()

    def have(*names):
        for name in names:
            for copy in loads.pop(name, []):
                copy.wait()

    def load_ring(i):
        name, at = (ACTIV, i) if i < 4 else (G_PRE, i - 4)
        start = (at % 2) * 1536 + (at // 2) * 768
        ring_loads[i] = pltpu.make_async_copy(
            hbm_in[name].at[:, pl.ds(start, 768)], ring.at[i % 3], ring_sem.at[i]
        )
        ring_loads[i].start()

    load(G_ATTN, CONTEXTS)
    if direct:
        bufs = [refs[7 * i : 7 * i + 7] for i in range(5)]
        refs = refs[35:]
        scatter = Scatter(SCATTER_CHUNKS, outs, bufs, *refs[:2])
        greet()
    mask_into(bias, marks)
    head_sum[...] = jnp.zeros_like(head_sum)

    def put(chunk, half, value):
        which, start, size = SCATTER_CHUNKS[chunk][:3]
        if direct:
            scatter.fill(chunk, half, value)
        elif which == 0:
            for kind in range(3):
                part = value[:, 128 * kind : 128 * (kind + 1)].astype(BF)
                outs[0][half, :, pl.ds(384 * kind + start, 128)] = part
        else:
            outs[which][half, :, pl.ds(start, size)] = value.astype(BF)

    def comm(piece, i=0):
        if direct:
            for at in FOLLOW.get((piece, i), ()):
                if at is LITTLE:
                    little.step()
                else:
                    scatter.phase(*at)

    tokens_t, g_attn_t = held[G_FFN_T], held[NORMED_T]
    have(G_ATTN, CONTEXTS)
    load(G_FFN_T)
    load_ring(0)
    load_ring(1)
    for i in range(blocks):
        rows = slice(i * ROW_BLOCK, (i + 1) * ROW_BLOCK)
        g_attn_t[:, rows] = jnp.transpose(held[G_ATTN][rows, :])
    for t in range(2):
        put(0, t, dot(g_attn_t[...], held[CONTEXTS][t]))
    if direct:
        met()
    comm(OUT)
    for i in range(8):
        left = held[G_FFN_T if i < 4 else NORMED_T]
        have(G_FFN_T if i < 4 else NORMED_T)
        ring_loads.pop(i).wait()
        if i == 0:
            load_ring(2)
            load(NORMED_T)
        if i == 2:
            load(OUT_W, MIX)
        if i == 4:
            load(TOKENS)
        if i == 6:
            load(QKV_W)
        put(1 + i // 2, i % 2, dot(left[...], ring[i % 3]))
        if i < 5:
            load_ring(i + 3)
        comm(FEED, i)

    have(OUT_W)

    @pl.loop(0, blocks)
    def _(i):
        rows = pl.ds(pl.multiple_of(i * ROW_BLOCK, ROW_BLOCK), ROW_BLOCK)
        for t in range(2):
            g_context[t, rows, :] = dot(held[G_ATTN][rows, :], held[OUT_W][t]).astype(BF)

    comm(CONTEXT)
    have(MIX, TOKENS)
    for i in range(blocks):
        rows = slice(i * ROW_BLOCK, (i + 1) * ROW_BLOCK)
        tokens_t[:, rows] = jnp.transpose(held[TOKENS][rows, :])
    begin = 0
    for end in range(12):
        if (PAIR, end) not in FOLLOW and end % 4 < 3:
            continue

        @pl.loop(begin, end + 1)
        def _(m):
            attend_back(m, held[MIX], bias, lse, g_context, affine, g_mix, head_sum)

        begin = end + 1
        if end % 4 == 3:
            comm(PAIR, end)
            col = end // 4
            if direct and col < 2:
                scatter.release(col)
            for t in range(2):
                put(5 + col, t, dot(tokens_t[...], g_mix[t, :, 384 * col : 384 * (col + 1)]))
            comm(QGRAD, col)
        else:
            comm(PAIR, end)

    small_in = small if not direct else refs[2].at[0]
    small_in[...] = small_a[...]
    ones = jnp.ones((8, rows_all), BF)
    for t in range(2):
        sums = dot(ones, g_mix[t])
        for col in range(3):
            at = slice(384 * t + 128 * col, 384 * t + 128 * (col + 1))
            small_in[17:18, at] = sums[0:1, 384 * col : 384 * col + 128]
            small_in[18:19, at] = sums[0:1, 384 * col + 256 : 384 * col + 384]
        at = slice(384 * t, 384 * (t + 1))
        small_in[19:20, at] = head_sum[t, 0:1, :] / affine[t, 1:2, 768:1152]
    if direct:
        little = Small(small, *refs[2:7])
        little.step()
    comm(SUMS)
    have(QKV_W)

    def resid_load(i):
        rows = pl.ds(i * ROW_BLOCK, ROW_BLOCK)
        return pltpu.make_async_copy(hbm_in[G_RESID].at[rows], resid.at[i % 2], resid_sem.at[i])

    def out_copy(i):
        rows = pl.ds(i * ROW_BLOCK, ROW_BLOCK)
        return pltpu.make_async_copy(grads_out.at[i % 2], tokens_grad.at[rows], out_sem.at[i])

    resid_load(0).start()
    for i in range(blocks):
        if i + 1 < blocks:
            resid_load(i + 1).start()
        resid_load(i).wait()
        if i >= 2:
            out_copy(i - 2).wait()
        rows = slice(i * ROW_BLOCK, (i + 1) * ROW_BLOCK)
        grads_out[i % 2] = resid[i % 2] + (
            dot(g_mix[0, rows, :], held[QKV_W][0], NT) + dot(g_mix[1, rows, :], held[QKV_W][1], NT)
        )
        out_copy(i).start()
        comm(ROWS, i)
    for i in range(max(0, blocks - 2), blocks):
        out_copy(i).wait()
    if direct:
        little.finish()
        scatter.finish()


HELD = (G_ATTN, CONTEXTS, G_FFN_T, NORMED_T, OUT_W, MIX, TOKENS, QKV_W)
LOADED = HELD + (ACTIV, G_PRE, G_RESID)


def backward_call(direct, affine, marks, lse, small_a, arrays):
    rows = arrays[TOKENS].shape[0]
    seqs = rows // SEQ_LEN
    blocks = rows // ROW_BLOCK
    scratch = [pltpu.VMEM(arrays[name].shape, arrays[name].dtype) for name in HELD]
    scratch += [
        pltpu.VMEM((3, rows, 768), BF),
        pltpu.VMEM((2, ROW_BLOCK, D), F32),
        pltpu.VMEM((2, ROW_BLOCK, D), F32),
        pltpu.VMEM((seqs, SEQ_LEN, SEQ_LEN), F32),
        pltpu.VMEM((2, rows, 384), BF),
        pltpu.VMEM((2, rows, 1152), BF),
        pltpu.VMEM((2, 8, 384), F32),
        pltpu.SemaphoreType.DMA((len(HELD),)),
        pltpu.SemaphoreType.DMA((9,)),
        pltpu.SemaphoreType.DMA((8,)),
        pltpu.SemaphoreType.DMA((blocks,)),
        pltpu.SemaphoreType.DMA((blocks,)),
    ]
    if direct:
        scratch += Scatter.scratch((768,) * 4 + (384,)) + Scatter.semaphores(SCATTER_CHUNKS)
        scratch += Small.scratch()
        extra = dict(collective_id=2, has_side_effects=True)
        grads = [jax.ShapeDtypeStruct((3, 48, 384), F32)]
        grads += [jax.ShapeDtypeStruct((48, w), F32) for w in WIDTHS[1:]]
    else:
        extra = {}
        grads = [jax.ShapeDtypeStruct((2, D, w), BF) for w in WIDTHS]
    tokens_grad, *grads, small = pl.pallas_call(
        functools.partial(backward_kernel, direct),
        out_shape=[
            jax.ShapeDtypeStruct((rows, D), F32),
            *grads,
            jax.ShapeDtypeStruct((SMALL_ROWS, D), F32),
        ],
        in_specs=vmem(4) + hbm(len(LOADED)),
        out_specs=hbm(1) + vmem(5),
        scratch_shapes=scratch,
        compiler_params=pltpu.CompilerParams(vmem_limit_bytes=VMEM_BYTES, **extra),
        name="backward",
    )(affine, marks, lse, small_a, *[arrays[name] for name in LOADED])
    return tokens_grad, grads, small


def finish_kernel(tokens_all, *refs):
    refs, moved = refs[:14] + refs[16:33], (refs[14:16], refs[33:35])
    for src, dst in zip(*moved):
        dst[...] = src[...]

    @pl.when(pl.program_id(0) == 0)
    def _():
        finish_small(tokens_all, *refs)


def finish_small(tokens_all, *refs):
    logits, noises = refs[:4], refs[4:8]
    scales, small = refs[8:10]
    grads, refs = refs[10:14], refs[14:]
    outs, refs = refs[:4], refs[4:]
    loss, qkv_b, out_b, up_b, down_b, gain1, shift1, gain2, shift2 = refs[:9]
    head, unit, width, layer = refs[9:]
    for src, dst in zip(grads, outs):
        dst[...] = src[...]
    zh, zu, zw, zl = (gate(flat_row(n), flat_row(v)) for n, v in zip(noises, logits))
    slope = lambda z: z * (1.0 - z) * 1.5

    def row(k):
        return small[k : k + 1, :]

    def put(ref, value):
        ref[...] = value.reshape(ref.shape)

    put(loss, jnp.sum(row(8), axis=1, keepdims=True) * (0.5 / tokens_all))
    qkv_b[...] = small[17:19, :]
    put(out_b, row(0) * scales[1:2, :])
    put(down_b, row(2) * scales[5:6, :])
    for k, ref in ((4, gain1), (5, shift1), (6, gain2), (7, shift2)):
        put(ref, row(k))
    put(up_b, jnp.concatenate([row(9 + j) for j in range(4)], axis=1))
    put(unit, jnp.concatenate([row(13 + j) for j in range(4)], axis=1) * slope(zu))
    put(width, (row(1) * zl[:, 0:1] + row(3) * zl[:, 1:2]) * slope(zw))
    at = lax.broadcasted_iota(jnp.int32, (1, 2), 1)
    first = jnp.sum(row(1) * zw, axis=1, keepdims=True)
    second = jnp.sum(row(3) * zw, axis=1, keepdims=True)
    put(layer, jnp.where(at == 0, first, second) * slope(zl))
    at = lax.broadcasted_iota(jnp.int32, (1, HEADS), 1)
    feature = lax.broadcasted_iota(jnp.int32, (1, D), 1) // HEAD_DIM
    total = jnp.zeros((1, HEADS), F32)
    for h in range(HEADS):
        mine = jnp.sum(jnp.where(feature == h, row(19), 0.0), axis=1, keepdims=True)
        total = jnp.where(at == h, mine, total)
    put(head, total * slope(zh))


def finish_call(tokens_all, raw, vec, small, grads, results):
    sizes = [1, 0, D, FF, D, D, D, D, D, HEADS, FF, D, 2]
    shapes = [jax.ShapeDtypeStruct(g.shape, F32) for g in grads]
    shapes += [jax.ShapeDtypeStruct((n,) if n else (2, D), F32) for n in sizes]
    by_rows = pl.BlockSpec((ROW_BLOCK, D), lambda i: (i, 0))

    def fixed(arrays):
        return [pl.BlockSpec(v.shape, lambda i, n=len(v.shape): (0,) * n) for v in arrays]

    ins = [*raw[LOGITS:], vec, small, *grads]
    return pl.pallas_call(
        functools.partial(finish_kernel, tokens_all),
        grid=(results[0].shape[0] // ROW_BLOCK,),
        out_shape=shapes + [jax.ShapeDtypeStruct(v.shape, v.dtype) for v in results],
        in_specs=fixed(ins) + [by_rows] * 2,
        out_specs=fixed(shapes) + [by_rows] * 2,
        name="finish",
    )(*ins, *results)


GATHER_CHUNKS = (
    (0, 0, 384, 0),
    (0, 384, 384, 0),
    (0, 768, 384, 0),
    (2, 0, 768, 0),
    (2, 768, 768, 0),
    (3, 0, 768, 0),
    (3, 768, 768, 0),
    (1, 0, 384, 1),
)
SCATTER_CHUNKS = (
    (1, 0, 384, 4, 0),
    (3, 0, 768, 0, 0),
    (3, 768, 768, 1, 0),
    (2, 0, 768, 2, 0),
    (2, 768, 768, 3, 0),
    (0, 0, 384, 4, 0),
    (0, 128, 384, 0, 0),
    (0, 256, 384, 0, 384),
)


def body(direct, tokens, teacher, segments, qkv_weight, qkv_bias, out_weight, out_bias, *args):
    up_weight, up_bias, down_weight, *args = args
    raw = (qkv_bias, out_bias, up_bias, *args)
    kinds = jnp.transpose(qkv_weight, (1, 0, 2))
    weights = [kinds, out_weight, up_weight, down_weight]
    if not direct:
        weights[0] = qkv_weight.reshape(-1, 1152)
        weights = [
            lax.all_gather(lax.all_gather(s, "dp", axis=0, tiled=True), "tensor", axis=0)
            for s in weights
        ]
    lse, affine, vec, small_a, arrays = forward_call(
        direct, tokens, teacher, segments, raw, weights
    )
    tokens_grad, grads, small = backward_call(direct, affine, segments, lse, small_a, arrays)
    if not direct:
        grads = [
            lax.psum_scatter(
                lax.psum_scatter(g, "tensor", scatter_dimension=0),
                "dp",
                scatter_dimension=0,
                tiled=True,
            ).astype(F32)
            for g in grads
        ]
        grads[0] = jnp.transpose(grads[0].reshape(-1, 3, 384), (1, 0, 2))
        small = lax.psum(small, ("dp", "tensor"))
    all_tokens = tokens.shape[0] * lax.axis_size("dp") * lax.axis_size("tensor")
    outs = finish_call(
        all_tokens, raw, vec, small, grads, (arrays[ACTIVATIONS], tokens_grad)
    )
    *outs, activations, tokens_grad = outs
    qkv_grad, out_grad, up_grad, down_grad, loss, qkv_b, out_b, up_b, down_b = outs[:9]
    return (
        activations,
        loss.reshape(()),
        tokens_grad,
        jnp.transpose(qkv_grad, (1, 0, 2)),
        qkv_b,
        out_grad,
        out_b,
        up_grad,
        up_b,
        down_grad,
        down_b,
        *outs[9:],
    )


def solution(mesh):
    rows, split, whole = P(("dp", "tensor"), None), P("dp", "tensor"), P()
    cube = P("dp", None, "tensor")
    in_specs = (rows, rows, rows, cube, whole, split, whole, split, whole, split) + (whole,) * 13
    out_specs = (
        rows,
        whole,
        rows,
        cube,
        whole,
        split,
        whole,
        split,
        whole,
        split,
    ) + (whole,) * 9
    direct = mesh.shape["dp"] == 16 and mesh.shape["tensor"] == 2
    return jax.shard_map(
        functools.partial(body, direct),
        mesh=mesh,
        in_specs=in_specs,
        out_specs=out_specs,
        check_vma=False,
    )
```
